256 devices in a mesh: ctx: 64 (over y, x_lo, z), dp: 4 (over x_hi, core).
Axes of the slice: x: 4 (x_hi: 2, x_lo: 2; x = x_hi * 2 + x_lo), y: 4, z: 8, core: 2. Of those that a mesh axis runs over, the one named last changes fastest.
Arguments:
- all_query_heads: bfloat16 [4, 8192, 4096], P('dp', 'ctx'), may hold values from -32 to 32
- grouped_key_heads: bfloat16 [4, 8192, 512], P('dp', 'ctx'), may hold values from -32 to 32
- grouped_value_heads: bfloat16 [4, 8192, 512], P('dp', 'ctx'), may hold values from -5 to 5
- output_gradient: bfloat16 [4, 8192, 4096], P('dp', 'ctx'), may hold values from -72 to 72
- head_ordering: int32 [4, 4], P('dp'), may hold values from 0 to 3, each once within a row
- adapter_activations: bfloat16 [4, 8192, 48], P('dp', 'ctx'), may hold values from -0.03125 to 0.03125
Outputs:
- query_gradient: bfloat16 [4, 8192, 4096], P('dp', 'ctx')
- key_gradient: bfloat16 [4, 8192, 512], P('dp', 'ctx')
- value_gradient: bfloat16 [4, 8192, 512], P('dp', 'ctx')
- adapter_query_gradient: float32 [16, 4096], P(None, ('ctx', 'dp'))
- adapter_key_value_gradient: float32 [16, 1024], P(None, ('ctx', 'dp'))
The draws below stay inside these ranges and needn't reach their ends.
Inputs may be any that keep to these rules, and one draw needn't show every extreme that they name: `head_ordering`: each row names each key-value head once.
All inputs are finite; a program needn't handle non-finite values.
Results may differ from the reference program's by a relative error of at most 0.017.
Values may be sent and summed in bfloat16 or wider, within the bound.
A program may use at most 64 MiB of HBM per device.

```python
import math
import jax
import jax.numpy as jnp
from jax import lax

KV_HEADS = 4
QUERY_SHARE = 8
HEAD_DIM = 128
ADAPTER_RANK = 16
HEADS = 32
SHIFTED = 2
GROUP = 2048
SEQUENCE_LENGTH = 8192
BATCH_COUNT = 4


def draw_all_query_heads(key, part):
    key = jax.random.fold_in(key, 7)
    array_dimensions = (BATCH_COUNT, SEQUENCE_LENGTH, KV_HEADS, QUERY_SHARE, HEAD_DIM)
    sample = jnp.clip(jax.random.normal(key, array_dimensions, jnp.float32), -5.0, 5.0)
    return sample.reshape(BATCH_COUNT, SEQUENCE_LENGTH, KV_HEADS * QUERY_SHARE * HEAD_DIM).astype(jnp.bfloat16)


def draw_grouped_key_heads(key, part):
    key = jax.random.fold_in(key, 11)
    array_dimensions = (BATCH_COUNT, SEQUENCE_LENGTH, KV_HEADS, HEAD_DIM)
    sample = jnp.clip(jax.random.normal(key, array_dimensions, jnp.float32), -5.0, 5.0)
    return sample.reshape(BATCH_COUNT, SEQUENCE_LENGTH, KV_HEADS * HEAD_DIM).astype(jnp.bfloat16)


def steps_of(own_key, extent, split, low, top_value):
    def one(dim, parts):
        draws = jax.random.uniform(jax.random.fold_in(jax.random.fold_in(own_key, 6), dim), (parts,), jnp.float32, low / len(split), top_value / len(split))
        return jnp.repeat(jnp.exp(draws), extent[dim] // parts).reshape((-1,) + (1,) * (len(extent) - dim - 1))

    factor_of = one(*split[0])
    for cut in split[1:]:
        factor_of = factor_of * one(*cut)
    return factor_of


def normal_values(key, extent, deviation, bound, shards=(), kind=jnp.bfloat16):
    result = jax.random.normal(key, extent, jnp.float32) * deviation
    if len(shards) > 0:
        result = steps_of(key, extent, shards, -0.22, 0.18) * result
    return jnp.clip(result, min=-bound, max=bound).astype(kind)


def setup_inputs(seed: int = 0) -> dict:
    key_of = jax.random.split(jax.random.key(seed), 7)
    all_query_heads = draw_all_query_heads(jax.random.fold_in(key_of[6], 71), 0)
    grouped_key_heads = draw_grouped_key_heads(jax.random.fold_in(key_of[6], 71), 0)
    grouped_value_heads = normal_values(key_of[2], (BATCH_COUNT, SEQUENCE_LENGTH, KV_HEADS * HEAD_DIM), 1.0, 5.0, ((0, 4), (1, 64)))
    output_gradient = normal_values(key_of[3], (BATCH_COUNT, SEQUENCE_LENGTH, HEADS * HEAD_DIM), 12.0, 72.0, ((0, 4), (1, 64)))
    head_ordering = jax.vmap(lambda own: jax.random.permutation(own, KV_HEADS))(jax.random.split(key_of[4], BATCH_COUNT)).reshape((BATCH_COUNT, KV_HEADS)).astype(jnp.int32)
    adapter_activations = normal_values(key_of[5], (BATCH_COUNT, SEQUENCE_LENGTH, 3 * ADAPTER_RANK), (SEQUENCE_LENGTH * BATCH_COUNT) ** -0.5, 0.03125, ((0, 4), (1, 64)))
    return dict(all_query_heads=all_query_heads, grouped_key_heads=grouped_key_heads, grouped_value_heads=grouped_value_heads, output_gradient=output_gradient, head_ordering=head_ordering, adapter_activations=adapter_activations)


def rounded(values):
    return lax.optimization_barrier(values.astype(jnp.bfloat16)).astype(jnp.float32)

def head_grads(pieces):
    queries, keys, values, grads_out = pieces
    score_scale = 1.0 / math.sqrt(HEAD_DIM)
    query_wide = queries.astype(jnp.float32)
    key_wide = keys.astype(jnp.float32)
    value_wide = values.astype(jnp.float32)
    grad_wide = grads_out.astype(jnp.float32)
    length = queries.shape[0]
    row_index = lax.broadcasted_iota(jnp.int32, (length, length), 0)
    col_index = lax.broadcasted_iota(jnp.int32, (length, length), 1)
    scores = jnp.einsum('tqd,ld->qtl', query_wide, key_wide) * score_scale
    masked = jnp.where(col_index <= row_index, scores, -jnp.inf)
    row_max = lax.optimization_barrier(jnp.max(masked, axis=-1, keepdims=True))
    row_total = lax.optimization_barrier(jnp.sum(jnp.exp(masked - row_max), axis=-1, keepdims=True))
    weights = jnp.exp(masked - (row_max + jnp.log(row_total)))
    dweights = jnp.einsum('tqd,ld->qtl', grad_wide, value_wide)
    row_delta = lax.optimization_barrier(jnp.sum(weights * dweights, axis=-1, keepdims=True))
    dscores = rounded(weights * (dweights - row_delta))
    weights_low = rounded(weights)
    grad_v = jnp.einsum('qtl,tqd->ld', weights_low, grad_wide)
    grad_k = jnp.einsum('qtl,tqd->ld', dscores, query_wide) * score_scale
    grad_q = jnp.einsum('qtl,ld->tqd', dscores, key_wide) * score_scale
    return (grad_q, grad_k, grad_v)

def group_grads(pieces):
    queries, keys, values, grads_out = pieces
    by_head = (jnp.moveaxis(queries, 1, 0), jnp.moveaxis(keys, 1, 0), jnp.moveaxis(values, 1, 0), jnp.moveaxis(grads_out, 1, 0))
    grad_q, grad_k, grad_v = lax.map(head_grads, by_head)
    return (jnp.moveaxis(grad_q, 0, 1), jnp.moveaxis(grad_k, 0, 1), jnp.moveaxis(grad_v, 0, 1))

def roll_shifted(array, offset):
    moved_heads = jnp.roll(array[:, :, :SHIFTED], offset, axis=1)
    return jnp.concatenate([moved_heads, array[:, :, SHIFTED:]], axis=2)

def reorder(array, ordering):
    return jax.vmap(lambda single, order: jnp.take(single, order, axis=1))(array, ordering)

def reference(all_query_heads, grouped_key_heads, grouped_value_heads, output_gradient, head_ordering, adapter_activations):
    half_group = GROUP // 2
    groups = SEQUENCE_LENGTH // GROUP
    queries = reorder(all_query_heads.reshape(BATCH_COUNT, SEQUENCE_LENGTH, KV_HEADS, QUERY_SHARE, HEAD_DIM), head_ordering)
    grads_out = reorder(output_gradient.reshape(BATCH_COUNT, SEQUENCE_LENGTH, KV_HEADS, QUERY_SHARE, HEAD_DIM), head_ordering)
    keys = reorder(grouped_key_heads.reshape(BATCH_COUNT, SEQUENCE_LENGTH, KV_HEADS, HEAD_DIM), head_ordering)
    values = reorder(grouped_value_heads.reshape(BATCH_COUNT, SEQUENCE_LENGTH, KV_HEADS, HEAD_DIM), head_ordering)
    rolled = [roll_shifted(array, -half_group) for array in (queries, keys, values, grads_out)]
    pieces = tuple((array.reshape((BATCH_COUNT * groups, GROUP) + array.shape[2:]) for array in rolled))
    grad_q, grad_k, grad_v = lax.map(group_grads, pieces)
    positions = jnp.arange(KV_HEADS, dtype=jnp.int32)
    matches = (head_ordering[:, :, None] == positions[None, None, :]).astype(jnp.int32)
    inverse = lax.optimization_barrier(jnp.sum(positions[None, :, None] * matches, axis=1)).astype(jnp.int32)

    def finish(array, width):
        whole = array.reshape((BATCH_COUNT, SEQUENCE_LENGTH) + array.shape[2:])
        whole = roll_shifted(whole, half_group)
        whole = reorder(whole, inverse)
        return whole.astype(jnp.bfloat16).reshape(BATCH_COUNT, SEQUENCE_LENGTH, width)
    query_gradient = finish(grad_q, HEADS * HEAD_DIM)
    key_gradient = finish(grad_k, KV_HEADS * HEAD_DIM)
    value_gradient = finish(grad_v, KV_HEADS * HEAD_DIM)
    hidden_inputs = adapter_activations.reshape(BATCH_COUNT * SEQUENCE_LENGTH, 3 * ADAPTER_RANK)
    flattened_query = query_gradient.reshape(BATCH_COUNT * SEQUENCE_LENGTH, HEADS * HEAD_DIM)
    flattened_key = key_gradient.reshape(BATCH_COUNT * SEQUENCE_LENGTH, KV_HEADS * HEAD_DIM)
    flattened_value = value_gradient.reshape(BATCH_COUNT * SEQUENCE_LENGTH, KV_HEADS * HEAD_DIM)
    adapter_query_gradient = jnp.dot(hidden_inputs[:, :ADAPTER_RANK].T, flattened_query, preferred_element_type=jnp.float32)
    adapter_key_value_gradient = jnp.concatenate([jnp.dot(hidden_inputs[:, ADAPTER_RANK:2 * ADAPTER_RANK].T, flattened_key, preferred_element_type=jnp.float32), jnp.dot(hidden_inputs[:, 2 * ADAPTER_RANK:].T, flattened_value, preferred_element_type=jnp.float32)], axis=1)
    return (query_gradient, key_gradient, value_gradient, adapter_query_gradient, adapter_key_value_gradient)
```

```python
import math

import jax
import jax.numpy as jnp
from jax import lax
from jax.experimental import pallas as pl
from jax.experimental.pallas import tpu as pltpu
from jax.sharding import PartitionSpec as P

MESH = pl.DeviceIdType.MESH
F32 = jnp.float32
BF16 = jnp.bfloat16
BLOCK = 128
KV_HEADS = 4
SHARE = 8
ROWS = SHARE * BLOCK
LINE = 8
RANK = 16
SCALE = 1.0 / math.sqrt(BLOCK)
EXP2_SCALE = SCALE / math.log(2.0)
HIDDEN = -1e30


def dot(a, b, a_dim, b_dim):
    return lax.dot_general(a, b, (((a_dim,), (b_dim,)), ((), ())), preferred_element_type=F32)


def kernel(
    order_ref,
    q_ref,
    k_ref,
    v_ref,
    g_ref,
    act_ref,
    dq_ref,
    dk_ref,
    dv_ref,
    aq_ref,
    akv_ref,
    own_kv,
    line_kv,
    prev_kv,
    qs,
    gs,
    top,
    total,
    accum,
    p_low,
    s_low,
    dq_t,
    part,
    prev_part,
    next_part,
    left_out,
    left_in,
    right_out,
    right_in,
    final,
    terms,
    stage1,
    terms2,
    stage2,
    terms3,
    stage3,
    load_sem,
    g_right_e,
    g_right_l,
    g_left_e,
    g_left_l,
    g_next,
    b_prev,
    b_left_e,
    b_left_l,
    b_right_e,
    b_right_l,
    a_sem1,
    a_sem2,
    a_sem3,
):
    ctx = lax.axis_index("ctx")
    dp = lax.axis_index("dp")
    z = lax.rem(ctx, LINE)
    line = ctx // LINE
    base = line * LINE
    left = base + lax.rem(z + LINE - 1, LINE)
    right = base + lax.rem(z + 1, LINE)
    after = lax.rem(line + 1, LINE) * LINE + z
    before = lax.rem(line + LINE - 1, LINE) * LINE + z

    def copy(src, dst, sems, index, target):
        return pltpu.make_async_remote_copy(
            src_ref=src,
            dst_ref=dst,
            send_sem=sems.at[0, index],
            recv_sem=sems.at[1, index],
            device_id=target,
            device_id_type=MESH,
        )

    def slot(by):
        return lax.rem(z + by + LINE, LINE)

    def right_e(s, block):
        view = line_kv.at[block, pl.ds(0, 4)]
        return copy(view, view, g_right_e, s - 1, {"ctx": right})

    def right_l(s, block):
        view = line_kv.at[block, pl.ds(4, 4)]
        return copy(view, view, g_right_l, s - 1, {"ctx": right})

    def left_e(s, block):
        view = line_kv.at[block, pl.ds(0, 4)]
        return copy(view, view, g_left_e, s - 1, {"ctx": left})

    def left_l(s, block):
        view = line_kv.at[block, pl.ds(4, 4)]
        return copy(view, view, g_left_l, s - 1, {"ctx": left})

    def to_next(index, block):
        return copy(
            line_kv.at[block, pl.ds(0, 4)], prev_kv.at[block], g_next, index, {"ctx": after}
        )

    def to_prev(index):
        return copy(prev_part.at[index], next_part.at[index], b_prev, index, {"ctx": before})

    def back_left(s, first, sems):
        return copy(
            left_out.at[s - 1, pl.ds(first, 4)],
            left_in.at[s - 1, pl.ds(first, 4)],
            sems,
            s - 1,
            {"ctx": left},
        )

    def back_right(s, first, sems):
        return copy(
            right_out.at[s - 1, pl.ds(first, 4)],
            right_in.at[s - 1, pl.ds(first, 4)],
            sems,
            s - 1,
            {"ctx": right},
        )

    def load(src, dst, row, h, r):
        return pltpu.make_async_copy(
            src.at[:, pl.ds((h * SHARE + r) * BLOCK, BLOCK)],
            dst.at[h, pl.ds(r * BLOCK, BLOCK), :],
            load_sem.at[row, h * SHARE + r],
        )

    for h in range(KV_HEADS):
        for r in range(SHARE):
            load(q_ref, qs, 0, h, r).start()
            load(g_ref, gs, 1, h, r).start()

    barrier = pltpu.get_barrier_semaphore()
    for by in range(1, LINE):
        pl.semaphore_signal(barrier, inc=1, device_id={"ctx": base + slot(by)}, device_id_type=MESH)
        pl.semaphore_signal(
            barrier,
            inc=1,
            device_id={"ctx": lax.rem(line + by, LINE) * LINE + z},
            device_id_type=MESH,
        )
    for by in range(1, 4):
        pl.semaphore_signal(
            barrier, inc=1, device_id={"dp": lax.rem(dp + by, 4)}, device_id_type=MESH
        )
    pl.semaphore_wait(barrier, 2 * (LINE - 1) + 3)

    swap = 2 * (1 - lax.rem(line, 2))
    ordering = [order_ref[0, lax.rem(j + swap, KV_HEADS)] for j in range(KV_HEADS)]
    places = []
    for h in range(KV_HEADS):
        place = jnp.int32(0)
        for j in range(1, KV_HEADS):
            place = jnp.maximum(place, jnp.where(ordering[j] == h, j, 0))
        places.append(place)

    for h in range(KV_HEADS):
        own_kv[h, 0] = k_ref[:, pl.ds(h * BLOCK, BLOCK)]
        own_kv[h, 1] = v_ref[:, pl.ds(h * BLOCK, BLOCK)]
    for j in range(KV_HEADS):
        line_kv[z, 2 * j] = own_kv[ordering[j], 0]
        line_kv[z, 2 * j + 1] = own_kv[ordering[j], 1]

    right_e(1, z).start()
    left_e(1, z).start()
    to_next(0, z).start()

    @pl.when(z < LINE - 1)
    def _():
        right_l(1, z).start()

    @pl.when(z <= 2)
    def _():
        left_l(1, z).start()

    top[...] = jnp.full(top.shape, HIDDEN, F32)
    total[...] = jnp.zeros(total.shape, F32)
    accum[...] = jnp.zeros(accum.shape, F32)
    dq_t[...] = jnp.zeros(dq_t.shape, F32)

    width = 2 * BLOCK

    def name(j):
        return order_ref[0, lax.rem(j + swap, KV_HEADS)]

    def scores(j, piece, keys, diagonal):
        q = qs[name(j), pl.ds(piece * width, width), :]
        s = dot(keys, q, 1, 1) * EXP2_SCALE
        if diagonal:
            key_at = lax.broadcasted_iota(jnp.int32, (BLOCK, width), 0)
            query_at = lax.rem(lax.broadcasted_iota(jnp.int32, (BLOCK, width), 1), BLOCK)
            own = jnp.where(key_at <= query_at, s[-BLOCK:], HIDDEN)
            s = own if s.shape[0] == BLOCK else jnp.concatenate([s[:-BLOCK], own], axis=0)
        return s

    def first_pass(j, keys, values, diagonal):
        for piece in range(ROWS // width):
            cols = pl.ds(piece * width, width)
            s = scores(j, piece, keys, diagonal)
            old = top[j, :, cols]
            new = jnp.maximum(old, jnp.max(s, axis=0, keepdims=True))
            e = jnp.exp2(s - new)
            dp_ = dot(values, gs[name(j), cols, :], 1, 1)
            factor = jnp.exp2(old - new)
            total[j, :, cols] = total[j, :, cols] * factor + jnp.sum(e, axis=0, keepdims=True)
            accum[j, :, cols] = accum[j, :, cols] * factor + jnp.sum(e * dp_, axis=0, keepdims=True)
            top[j, :, cols] = new

    def second_pass(j, keys, values, diagonal):
        count = keys.shape[0]
        for piece in range(ROWS // width):
            cols = pl.ds(piece * width, width)
            p = jnp.exp2(scores(j, piece, keys, diagonal) - top[j, :, cols])
            dp_ = dot(values, gs[name(j), cols, :], 1, 1)
            s_low[pl.ds(0, count), cols] = (p * (dp_ - accum[j, :, cols])).astype(BF16)
            p_low[pl.ds(0, count), cols] = p.astype(BF16)
        ds = s_low[pl.ds(0, count), :]
        dk = dot(ds, qs[name(j)], 1, 0)
        dv = dot(p_low[pl.ds(0, count), :], gs[name(j)], 1, 0)
        dq_t[j] += dot(keys, ds, 0, 0)
        return dk, dv

    def own_keys(j, blocks):
        keys = [line_kv[b, 2 * j] for b in blocks]
        values = [line_kv[b, 2 * j + 1] for b in blocks]
        if len(blocks) == 1:
            return keys[0], values[0]
        return jnp.concatenate(keys, axis=0), jnp.concatenate(values, axis=0)

    def prev_keys(j, blocks):
        keys = [prev_kv[b, 2 * j] for b in blocks]
        values = [prev_kv[b, 2 * j + 1] for b in blocks]
        return jnp.concatenate(keys, axis=0), jnp.concatenate(values, axis=0)

    def own_cases(t, run):
        far = 9 - t

        @pl.when((t == 1) & (z >= 1))
        def _():
            run((1, 0), True)

        @pl.when((t == 1) & (z == 0))
        def _():
            run((0,), True)

        @pl.when((t > 1) & (z >= far))
        def _():
            run((t, far), False)

        @pl.when((t > 1) & (z >= t) & (z < far))
        def _():
            run((t,), False)

    def prev_pair(t):
        second = jnp.where(t == 1, 0, 2 * t - 2)
        return (2 * t - 1, second), (slot(-t), lax.rem(z + t - 1, LINE))

    def gather_step(t, carry):
        block = slot(-t)
        right_e(t, block).wait_recv()

        @pl.when(t < 4)
        def _():
            right_e(t + 1, block).start()

        to_next(2 * t - 1, block).start()

        @pl.when(t < 4)
        def _():
            other = slot(t)
            left_e(t, other).wait_recv()

            @pl.when(t < 3)
            def _():
                left_e(t + 1, other).start()

            to_next(2 * t, other).start()

            @pl.when(other <= 2)
            def _():
                left_l(t, other).wait_recv()

                @pl.when(t < 3)
                def _():
                    left_l(t + 1, other).start()

        @pl.when(z >= t)
        def _():
            right_l(t, block).wait_recv()

            @pl.when((t < 4) & (z < LINE - 1))
            def _():
                right_l(t + 1, block).start()

        def run(distances, diagonal):
            blocks = [slot(-d) for d in distances]

            def head(j, c):
                keys, values = own_keys(j, blocks)
                first_pass(j, keys, values, diagonal)
                return c

            lax.fori_loop(0, KV_HEADS, head, 0)

        own_cases(t, run)
        indices, blocks = prev_pair(t)
        for index, b in zip(indices, blocks):
            to_next(index, b).wait_recv()

        def head(j, c):
            keys, values = prev_keys(j, blocks)
            first_pass(j + 2, keys, values, False)
            return c

        lax.fori_loop(0, 2, head, 0)
        return carry

    for h in range(KV_HEADS):
        for r in range(SHARE):
            load(q_ref, qs, 0, h, r).wait()
            load(g_ref, gs, 1, h, r).wait()
    lax.fori_loop(1, 5, gather_step, 0)

    top[...] = top[...] + jnp.log2(total[...])
    accum[...] = accum[...] / total[...]

    def prev_step(t):
        indices, blocks = prev_pair(t)

        def head(j, c):
            keys, values = prev_keys(j, blocks)
            dk, dv = second_pass(j + 2, keys, values, False)
            for i, index in enumerate(indices):
                rows = slice(i * BLOCK, (i + 1) * BLOCK)
                prev_part[index, 2 * j] = dk[rows].astype(BF16)
                prev_part[index, 2 * j + 1] = dv[rows].astype(BF16)
            return c

        lax.fori_loop(0, 2, head, 0)
        for index in indices:
            to_prev(index).start()

    def own_step(t):
        far = jnp.where(t == 1, 0, 9 - t)

        @pl.when(z < far)
        def _():
            part[far] = jnp.zeros(part.shape[1:], F32)

        @pl.when(z < t)
        def _():
            part[t] = jnp.zeros(part.shape[1:], F32)

        def run(distances, diagonal):
            blocks = [slot(-d) for d in distances]

            def head(j, c):
                keys, values = own_keys(j, blocks)
                dk, dv = second_pass(j, keys, values, diagonal)
                for i, d in enumerate(distances):
                    rows = slice(i * BLOCK, (i + 1) * BLOCK)
                    part[d, 2 * j] = dk[rows]
                    part[d, 2 * j + 1] = dv[rows]
                return c

            lax.fori_loop(0, KV_HEADS, head, 0)

        own_cases(t, run)

    early, late = pl.ds(0, 4), pl.ds(4, 4)

    def flush(t):
        @pl.when(t < 4)
        def _():
            back_left(t + 1, 0, b_left_e).wait_recv()
            part[t, early] += left_in[t, early].astype(F32)

        to_prev(2 * t - 1).wait_recv()
        left_out[t - 1, early] = (part[t, early] + next_part[2 * t - 1].astype(F32)).astype(BF16)
        back_left(t, 0, b_left_e).start()

        @pl.when(z >= t)
        def _():
            @pl.when((t < 4) & (z < LINE - 1))
            def _():
                back_left(t + 1, 4, b_left_l).wait_recv()
                part[t, late] += left_in[t, late].astype(F32)

            left_out[t - 1, late] = part[t, late].astype(BF16)
            back_left(t, 4, b_left_l).start()

        @pl.when(t > 1)
        def _():
            s = t - 1
            far = 9 - t

            @pl.when(t < 4)
            def _():
                back_right(s + 1, 0, b_right_e).wait_recv()
                part[far, early] += right_in[s, early].astype(F32)

            to_prev(2 * s).wait_recv()
            right_out[s - 1, early] = (part[far, early] + next_part[2 * s].astype(F32)).astype(BF16)
            back_right(s, 0, b_right_e).start()

            @pl.when(slot(s) <= 2)
            def _():
                @pl.when(t < 4)
                def _():
                    back_right(s + 1, 4, b_right_l).wait_recv()
                    part[far, late] += right_in[s, late].astype(F32)

                right_out[s - 1, late] = part[far, late].astype(BF16)
                back_right(s, 4, b_right_l).start()

    prev_step(4)

    def back_step(i, carry):
        t = 4 - i

        @pl.when(t > 1)
        def _():
            prev_step(t - 1)

        own_step(t)
        flush(t)
        return carry

    lax.fori_loop(0, 4, back_step, 0)

    for h in range(KV_HEADS):
        for r in range(SHARE):
            block = dq_t[places[h], :, pl.ds(r * BLOCK, BLOCK)] * SCALE
            dq_ref[:, pl.ds((h * SHARE + r) * BLOCK, BLOCK)] = block.astype(BF16).T
    for c in range(LINE):
        terms[c, :, pl.ds(0, 512)] = dot(
            act_ref[:, 0:RANK], dq_ref[:, pl.ds(c * 512, 512)], 0, 0
        )

    to_prev(0).wait_recv()
    back_left(1, 0, b_left_e).wait_recv()
    back_right(1, 0, b_right_e).wait_recv()
    final[early] = (
        part[0, early]
        + next_part[0].astype(F32)
        + left_in[0, early].astype(F32)
        + right_in[0, early].astype(F32)
    )
    final[late] = part[0, late]

    @pl.when(z < LINE - 1)
    def _():
        back_left(1, 4, b_left_l).wait_recv()
        final[late] += left_in[0, late].astype(F32)

    @pl.when(z <= 2)
    def _():
        back_right(1, 4, b_right_l).wait_recv()
        final[late] += right_in[0, late].astype(F32)

    for h in range(KV_HEADS):
        columns = pl.ds(h * BLOCK, BLOCK)
        dk_ref[:, columns] = (final[2 * places[h]] * SCALE).astype(BF16)
        dv_ref[:, columns] = final[2 * places[h] + 1].astype(BF16)
    for h in range(KV_HEADS):
        columns = pl.ds(h * BLOCK, BLOCK)
        terms[h, :, pl.ds(512, BLOCK)] = dot(
            act_ref[:, RANK : 2 * RANK], dk_ref[:, columns], 0, 0
        )
        terms[KV_HEADS + h, :, pl.ds(512, BLOCK)] = dot(
            act_ref[:, 2 * RANK : 3 * RANK], dv_ref[:, columns], 0, 0
        )

    def stage1_copy(by):
        other = lax.rem(line + by, LINE)
        return copy(
            terms.at[other], stage1.at[by - 1], a_sem1, by - 1, {"ctx": other * LINE + z}
        )

    def stage2_copy(by):
        other = slot(by)
        return copy(
            terms2.at[other // 2], stage2.at[by - 1], a_sem2, by - 1, {"ctx": base + other}
        )

    def stage3_copy(by):
        return copy(terms3, stage3.at[by - 1], a_sem3, by - 1, {"dp": lax.rem(dp + by, 4)})

    for by in range(1, LINE):
        stage1_copy(by).start()
    value = terms[line]
    for by in range(1, LINE):
        stage1_copy(by).wait_recv()
        value = value + stage1[by - 1]
    for c in range(4):
        terms2[c, :, pl.ds(0, BLOCK)] = value[:, c * BLOCK : (c + 1) * BLOCK]
        terms2[c, :, pl.ds(BLOCK, BLOCK)] = value[:, 4 * BLOCK :]
    for by in range(1, LINE):
        stage2_copy(by).start()
    value = terms2[z // 2]
    for by in range(1, LINE):
        stage2_copy(by).wait_recv()
        value = value + stage2[by - 1]
    terms3[...] = value
    for by in range(1, 4):
        stage3_copy(by).start()
    for by in range(1, 4):
        stage3_copy(by).wait_recv()
        value = value + stage3[by - 1]
    q_first = lax.rem(z, 2) * 64 + dp * 16
    kv_first = z * 16 + dp * 4
    aq_ref[...] = pltpu.roll(value[:, :BLOCK], lax.rem(BLOCK - q_first, BLOCK), 1)[:, :16]
    akv_ref[...] = pltpu.roll(value[:, BLOCK:], lax.rem(BLOCK - kv_first, BLOCK), 1)[:, :4]

    for s in range(1, 5):
        block = slot(1 - s)
        right_e(s, block).wait_send()
        back_left(s, 0, b_left_e).wait_send()

        @pl.when((z >= s - 1) & (z < LINE - 1))
        def _():
            right_l(s, block).wait_send()

        @pl.when(z >= s)
        def _():
            back_left(s, 4, b_left_l).wait_send()

    for s in range(1, 4):
        block = slot(s - 1)
        left_e(s, block).wait_send()
        back_right(s, 0, b_right_e).wait_send()

        @pl.when(block <= 2)
        def _():
            left_l(s, block).wait_send()

        @pl.when(slot(s) <= 2)
        def _():
            back_right(s, 4, b_right_l).wait_send()

    for index in range(LINE):
        to_next(index, z).wait_send()
        to_prev(index).wait_send()
    for by in range(1, LINE):
        stage1_copy(by).wait_send()
        stage2_copy(by).wait_send()
    for by in range(1, 4):
        stage3_copy(by).wait_send()


def on_device(queries, keys, values, grads_out, ordering, activations):
    count = queries.shape[1]
    vmem = pl.BlockSpec(memory_space=pltpu.VMEM)
    hbm = pl.BlockSpec(memory_space=pl.ANY)
    pair = (2 * KV_HEADS, BLOCK, BLOCK)
    half = (KV_HEADS, BLOCK, BLOCK)

    def sems(n):
        return pltpu.SemaphoreType.DMA((2, n))

    dq, dk, dv, aq, akv = pl.pallas_call(
        kernel,
        out_shape=(
            jax.ShapeDtypeStruct((count, queries.shape[2]), BF16),
            jax.ShapeDtypeStruct((count, keys.shape[2]), BF16),
            jax.ShapeDtypeStruct((count, values.shape[2]), BF16),
            jax.ShapeDtypeStruct((RANK, 16), F32),
            jax.ShapeDtypeStruct((RANK, 4), F32),
        ),
        in_specs=[pl.BlockSpec(memory_space=pltpu.SMEM), hbm, vmem, vmem, hbm, vmem],
        out_specs=(vmem,) * 5,
        scratch_shapes=[
            pltpu.VMEM((KV_HEADS, 2, BLOCK, BLOCK), BF16),
            pltpu.VMEM((LINE,) + pair, BF16),
            pltpu.VMEM((LINE,) + half, BF16),
            pltpu.VMEM((KV_HEADS, ROWS, BLOCK), BF16),
            pltpu.VMEM((KV_HEADS, ROWS, BLOCK), BF16),
            pltpu.VMEM((KV_HEADS, 1, ROWS), F32),
            pltpu.VMEM((KV_HEADS, 1, ROWS), F32),
            pltpu.VMEM((KV_HEADS, 1, ROWS), F32),
            pltpu.VMEM((2 * BLOCK, ROWS), BF16),
            pltpu.VMEM((2 * BLOCK, ROWS), BF16),
            pltpu.VMEM((KV_HEADS, BLOCK, ROWS), F32),
            pltpu.VMEM((LINE,) + pair, F32),
            pltpu.VMEM((LINE,) + half, BF16),
            pltpu.VMEM((LINE,) + half, BF16),
            pltpu.VMEM((4,) + pair, BF16),
            pltpu.VMEM((4,) + pair, BF16),
            pltpu.VMEM((3,) + pair, BF16),
            pltpu.VMEM((3,) + pair, BF16),
            pltpu.VMEM(pair, F32),
            pltpu.VMEM((LINE, RANK, 5 * BLOCK), F32),
            pltpu.VMEM((LINE - 1, RANK, 5 * BLOCK), F32),
            pltpu.VMEM((4, RANK, 2 * BLOCK), F32),
            pltpu.VMEM((LINE - 1, RANK, 2 * BLOCK), F32),
            pltpu.VMEM((RANK, 2 * BLOCK), F32),
            pltpu.VMEM((3, RANK, 2 * BLOCK), F32),
            sems(KV_HEADS * SHARE),
            sems(4),
            sems(4),
            sems(3),
            sems(3),
            sems(LINE),
            sems(LINE),
            sems(4),
            sems(4),
            sems(3),
            sems(3),
            sems(LINE - 1),
            sems(LINE - 1),
            sems(3),
        ],
        compiler_params=pltpu.CompilerParams(
            collective_id=0, has_side_effects=True, vmem_limit_bytes=48 << 20
        ),
    )(ordering, queries[0], keys[0], values[0], grads_out[0], activations[0])
    return dq[None], dk[None], dv[None], aq, akv


def solution(mesh):
    placed = (
        P("dp", "ctx", None),
        P("dp", "ctx", None),
        P("dp", "ctx", None),
        P("dp", "ctx", None),
        P("dp", None),
        P("dp", "ctx", None),
    )
    return jax.shard_map(
        on_device,
        mesh=mesh,
        in_specs=placed,
        out_specs=(
            P("dp", "ctx", None),
            P("dp", "ctx", None),
            P("dp", "ctx", None),
            P(None, ("ctx", "dp")),
            P(None, ("ctx", "dp")),
        ),
        check_vma=False,
    )
```

```python
import math

import jax
import jax.numpy as jnp
from jax import lax
from jax.experimental import pallas as pl
from jax.experimental.pallas import tpu as pltpu
from jax.sharding import PartitionSpec as P

MESH = pl.DeviceIdType.MESH
F32 = jnp.float32
BF16 = jnp.bfloat16
BLOCK = 128
KV_HEADS = 4
SHARE = 8
ROWS = SHARE * BLOCK
AHEAD = 2
LINE = 8
RANK = 16
SCALE = 1.0 / math.sqrt(BLOCK)
EXP2_SCALE = SCALE / math.log(2.0)
HIDDEN = -1e30
ACT = 2 * RANK
HALF = 4 * BLOCK
EARLY = ACT + HALF
CHUNKS = ((0, ACT + 2 * BLOCK), (ACT + 2 * BLOCK, 2 * BLOCK))


def dot(a, b, a_dim, b_dim):
    return lax.dot_general(a, b, (((a_dim,), (b_dim,)), ((), ())), preferred_element_type=F32)


def kernel(
    order_ref,
    q_ref,
    k_ref,
    v_ref,
    g_ref,
    act_ref,
    dq_ref,
    dk_ref,
    dv_ref,
    aq_ref,
    akv_ref,
    own_kv,
    line_kv,
    prev_kv,
    qs,
    gs,
    acts,
    top,
    total,
    accum,
    p_low,
    s_low,
    dq_t,
    kv_terms,
    part,
    prev_part,
    next_part,
    left_out,
    left_in,
    right_out,
    right_in,
    final,
    terms,
    stage1,
    terms2,
    stage2,
    terms3,
    stage3,
    columns,
    load_sem,
    kv_sem,
    act_sem,
    g_right_e,
    g_right_l,
    g_left_e,
    g_left_l,
    g_next,
    b_prev,
    b_left_e,
    b_left_l,
    b_right_e,
    b_right_l,
    a_sem1,
    a_sem2,
    a_sem3,
):
    ctx = lax.axis_index("ctx")
    dp = lax.axis_index("dp")
    z = lax.rem(ctx, LINE)
    line = ctx // LINE
    base = line * LINE
    left = base + lax.rem(z + LINE - 1, LINE)
    right = base + lax.rem(z + 1, LINE)
    after = lax.rem(line + 1, LINE) * LINE + z
    before = lax.rem(line + LINE - 1, LINE) * LINE + z

    def copy(src, dst, sems, index, target):
        return pltpu.make_async_remote_copy(
            src_ref=src,
            dst_ref=dst,
            send_sem=sems.at[0, index],
            recv_sem=sems.at[1, index],
            device_id=target,
            device_id_type=MESH,
        )

    def slot(by):
        return lax.rem(z + by + LINE, LINE)

    def right_e(s, c, block):
        view = line_kv.at[block, pl.ds(*CHUNKS[c])]
        return copy(view, view, g_right_e, 2 * (s - 1) + c, {"ctx": right})

    def right_l(s, block):
        view = line_kv.at[block, pl.ds(EARLY, HALF)]
        return copy(view, view, g_right_l, s - 1, {"ctx": right})

    def left_e(s, c, block):
        view = line_kv.at[block, pl.ds(*CHUNKS[c])]
        return copy(view, view, g_left_e, 2 * (s - 1) + c, {"ctx": left})

    def left_l(s, block):
        view = line_kv.at[block, pl.ds(EARLY, HALF)]
        return copy(view, view, g_left_l, s - 1, {"ctx": left})

    def to_next(index, c, block):
        rows = pl.ds(*CHUNKS[c])
        return copy(
            line_kv.at[block, rows],
            prev_kv.at[block, rows],
            g_next,
            2 * index + c,
            {"ctx": after},
        )

    def to_prev(index, c):
        view = pl.ds(2 * c, 2)
        return copy(
            prev_part.at[index, view],
            next_part.at[index, view],
            b_prev,
            2 * index + c,
            {"ctx": before},
        )

    def back_left_e(s, c):
        view = pl.ds(2 * c, 2)
        return copy(
            left_out.at[s - 1, view],
            left_in.at[s - 1, view],
            b_left_e,
            2 * (s - 1) + c,
            {"ctx": left},
        )

    def back_right_e(s, c):
        view = pl.ds(2 * c, 2)
        return copy(
            right_out.at[s - 1, view],
            right_in.at[s - 1, view],
            b_right_e,
            2 * (s - 1) + c,
            {"ctx": right},
        )

    def back_left_l(s):
        return copy(
            left_out.at[s - 1, pl.ds(4, 4)],
            left_in.at[s - 1, pl.ds(4, 4)],
            b_left_l,
            s - 1,
            {"ctx": left},
        )

    def back_right_l(s):
        return copy(
            right_out.at[s - 1, pl.ds(4, 4)],
            right_in.at[s - 1, pl.ds(4, 4)],
            b_right_l,
            s - 1,
            {"ctx": right},
        )

    def load(src, dst, row, h):
        return pltpu.make_async_copy(
            src.at[:, pl.ds(h * ROWS, ROWS)], dst.at[h], load_sem.at[row, h]
        )

    def load_kv(src, which, h):
        return pltpu.make_async_copy(
            src.at[:, pl.ds(h * BLOCK, BLOCK)], own_kv.at[h, which], kv_sem.at[which, h]
        )

    barrier = pltpu.get_barrier_semaphore()
    for by in range(1, LINE):
        pl.semaphore_signal(barrier, inc=1, device_id={"ctx": base + slot(by)}, device_id_type=MESH)
        pl.semaphore_signal(
            barrier,
            inc=1,
            device_id={"ctx": lax.rem(line + by, LINE) * LINE + z},
            device_id_type=MESH,
        )
    for by in range(1, 4):
        pl.semaphore_signal(
            barrier, inc=1, device_id={"dp": lax.rem(dp + by, 4)}, device_id_type=MESH
        )

    load_act = pltpu.make_async_copy(act_ref, acts, act_sem.at[0])
    for h in range(KV_HEADS):
        load_kv(k_ref, 0, h).start()
        load_kv(v_ref, 1, h).start()
    load_act.start()

    swap = 2 * (1 - lax.rem(line, 2))
    ordering = [order_ref[0, lax.rem(j + swap, KV_HEADS)] for j in range(KV_HEADS)]
    places = []
    for h in range(KV_HEADS):
        place = jnp.int32(0)
        for j in range(1, KV_HEADS):
            place = jnp.maximum(place, jnp.where(ordering[j] == h, j, 0))
        places.append(place)

    for h in range(KV_HEADS):
        load_kv(k_ref, 0, h).wait()
        load_kv(v_ref, 1, h).wait()
    load_act.wait()
    line_kv[z, pl.ds(0, ACT), :] = acts[pl.ds(RANK, ACT), :]
    for j in range(KV_HEADS):
        first = ACT + 2 * j * BLOCK
        line_kv[z, pl.ds(first, BLOCK), :] = own_kv[ordering[j], 0]
        line_kv[z, pl.ds(first + BLOCK, BLOCK), :] = own_kv[ordering[j], 1]

    pl.semaphore_wait(barrier, 2 * (LINE - 1) + 3)
    for c in range(2):
        left_e(1, c, z).start()
        right_e(1, c, z).start()
        to_next(0, c, z).start()

    for h in range(KV_HEADS):
        load(q_ref, qs, 0, h).start()
        load(g_ref, gs, 1, h).start()

    width = 2 * BLOCK

    def name(j):
        return order_ref[0, lax.rem(j + swap, KV_HEADS)]

    def rows_of(source, j, first, count):
        heads = [source[name(j), :, pl.ds(r * BLOCK, BLOCK)] for r in range(first, first + count)]
        return jnp.concatenate(heads, axis=0)

    def scores(j, piece, keys, diagonal):
        q = rows_of(qs, j, 2 * piece, 2)
        s = dot(keys, q, 1, 1) * EXP2_SCALE
        if diagonal:
            key_at = lax.broadcasted_iota(jnp.int32, (BLOCK, width), 0)
            query_at = lax.rem(lax.broadcasted_iota(jnp.int32, (BLOCK, width), 1), BLOCK)
            own = jnp.where(key_at <= query_at, s[-BLOCK:], HIDDEN)
            s = own if s.shape[0] == BLOCK else jnp.concatenate([s[:-BLOCK], own], axis=0)
        return s

    def first_pass(j, keys, values, diagonal):
        for piece in range(ROWS // width):
            cols = pl.ds(piece * width, width)
            s = scores(j, piece, keys, diagonal)
            old = top[j, :, cols]
            new = jnp.maximum(old, jnp.max(s, axis=0, keepdims=True))
            e = jnp.exp2(s - new)
            dp_ = dot(values, rows_of(gs, j, 2 * piece, 2), 1, 1)
            factor = jnp.exp2(old - new)
            total[j, :, cols] = total[j, :, cols] * factor + jnp.sum(e, axis=0, keepdims=True)
            accum[j, :, cols] = accum[j, :, cols] * factor + jnp.sum(e * dp_, axis=0, keepdims=True)
            top[j, :, cols] = new

    def second_pass(j, keys, values, acts_k, acts_v, diagonal):
        count = keys.shape[0]
        for piece in range(ROWS // width):
            cols = pl.ds(piece * width, width)
            p = jnp.exp2(scores(j, piece, keys, diagonal) - top[j, :, cols])
            dp_ = dot(values, rows_of(gs, j, 2 * piece, 2), 1, 1)
            s_low[pl.ds(0, count), cols] = (p * (dp_ - accum[j, :, cols])).astype(BF16)
            p_low[pl.ds(0, count), cols] = p.astype(BF16)
        ds = s_low[pl.ds(0, count), :]
        dk = dot(ds, rows_of(qs, j, 0, SHARE), 1, 0)
        dv = dot(p_low[pl.ds(0, count), :], rows_of(gs, j, 0, SHARE), 1, 0)
        dq_t[j] += dot(keys, ds, 0, 0)
        kv_terms[2 * j] += dot(acts_k, dk.astype(BF16), 1, 0)
        kv_terms[2 * j + 1] += dot(acts_v, dv.astype(BF16), 1, 0)
        return dk, dv

    def keys_of(source, j, blocks):
        first = pl.multiple_of(ACT + 2 * j * BLOCK, ACT)
        keys = [source[b, pl.ds(first, BLOCK), :] for b in blocks]
        values = [source[b, pl.ds(first + BLOCK, BLOCK), :] for b in blocks]
        if len(blocks) == 1:
            return keys[0], values[0]
        return jnp.concatenate(keys, axis=0), jnp.concatenate(values, axis=0)

    def acts_of(source, blocks):
        sides = [source[b, pl.ds(0, ACT), :] for b in blocks]
        both = sides[0] if len(blocks) == 1 else jnp.concatenate(sides, axis=1)
        return both[:RANK], both[RANK:]

    def own_cases(t, run):
        far = 9 - t

        @pl.when((t == 1) & (z >= 1))
        def _():
            run((1, 0), True)

        @pl.when((t == 1) & (z == 0))
        def _():
            run((0,), True)

        @pl.when((t > 1) & (z >= far))
        def _():
            run((t, far), False)

        @pl.when((t > 1) & (z >= t) & (z < far))
        def _():
            run((t,), False)

    def prev_pair(t):
        second = jnp.where(t == 1, 0, 2 * t - 2)
        return (2 * t - 1, second), (slot(-t), lax.rem(z + t - 1, LINE))

    def own_first(t, first):
        def run(distances, diagonal):
            blocks = [slot(-d) for d in distances]

            def head(j, c):
                keys, values = keys_of(line_kv, j, blocks)
                first_pass(j, keys, values, diagonal)
                return c

            lax.fori_loop(first, first + 2, head, 0)

        own_cases(t, run)

    def prev_first(t):
        indices, blocks = prev_pair(t)
        for index, b in zip(indices, blocks):
            for c in range(2):
                to_next(index, c, b).wait_recv()

        def head(j, c):
            keys, values = keys_of(prev_kv, j, blocks)
            first_pass(j + 2, keys, values, False)
            return c

        lax.fori_loop(0, 2, head, 0)

    def early_step(t):
        block = slot(-t)
        other = slot(t)
        for c in range(2):
            left_e(t, c, other).wait_recv()

            @pl.when(t < 4)
            def _():
                left_e(t + 1, c, other).start()

            to_next(jnp.minimum(2 * t, LINE - 1), c, other).start()

            @pl.when(t < 4)
            def _():
                right_e(t, c, block).wait_recv()

                @pl.when(t < 3)
                def _():
                    right_e(t + 1, c, block).start()

                to_next(2 * t - 1, c, block).start()

    def late_step(t):
        @pl.when(z >= t)
        def _():
            @pl.when(t > 0)
            def _():
                right_l(t, slot(-t)).wait_recv()

            @pl.when((t < 4) & (z < LINE - 1))
            def _():
                right_l(t + 1, slot(-t)).start()

        @pl.when((t < 4) & (slot(t) <= 2))
        def _():
            @pl.when(t > 0)
            def _():
                left_l(t, slot(t)).wait_recv()

            @pl.when(t < 3)
            def _():
                left_l(t + 1, slot(t)).start()

    def begin():
        top[...] = jnp.full(top.shape, HIDDEN, F32)
        total[...] = jnp.zeros(total.shape, F32)
        accum[...] = jnp.zeros(accum.shape, F32)
        dq_t[...] = jnp.zeros(dq_t.shape, F32)
        kv_terms[...] = jnp.zeros(kv_terms.shape, F32)
        for d in range(LINE):
            part[d] = jnp.zeros(part.shape[1:], F32)
        for h in range(KV_HEADS):
            load(q_ref, qs, 0, h).wait()
            load(g_ref, gs, 1, h).wait()

    def gather_step(t, carry):
        early_step(t)

        @pl.when(t == 1)
        def _():
            begin()

        def halves(u, c):
            @pl.when(u == 1)
            def _():
                late_step(t)

            own_first(t, 2 * u)
            return c

        lax.fori_loop(0, 2, halves, 0)

        @pl.when(t > 1)
        def _():
            prev_first(t - 1)

        return carry

    late_step(0)
    lax.fori_loop(1, 5, gather_step, 0)

    def close_rows(first):
        heads = pl.ds(first, 2)
        top[heads] = top[heads] + jnp.log2(total[heads])
        accum[heads] = accum[heads] / total[heads]

    def own_second(t, first):
        def run(distances, diagonal):
            blocks = [slot(-d) for d in distances]
            acts_k, acts_v = acts_of(line_kv, blocks)

            def head(j, c):
                keys, values = keys_of(line_kv, j, blocks)
                dk, dv = second_pass(j, keys, values, acts_k, acts_v, diagonal)
                for i, d in enumerate(distances):
                    rows = slice(i * BLOCK, (i + 1) * BLOCK)
                    part[d, 2 * j] = dk[rows]
                    part[d, 2 * j + 1] = dv[rows]
                return c

            lax.fori_loop(first, first + 2, head, 0)

        own_cases(t, run)

    def prev_second(t):
        indices, blocks = prev_pair(t)
        acts_k, acts_v = acts_of(prev_kv, blocks)

        def head(j, c):
            keys, values = keys_of(prev_kv, j, blocks)
            dk, dv = second_pass(j + 2, keys, values, acts_k, acts_v, False)
            for i, index in enumerate(indices):
                rows = slice(i * BLOCK, (i + 1) * BLOCK)
                prev_part[index, 2 * j] = dk[rows].astype(BF16)
                prev_part[index, 2 * j + 1] = dv[rows].astype(BF16)
            return c

        lax.fori_loop(0, 2, head, 0)
        for index in indices:
            for c in range(2):
                to_prev(index, c).start()

    late = pl.ds(4, 4)

    def flush(t):
        ahead = LINE - t

        @pl.when(z >= t)
        def _():
            @pl.when((t < 4) & (z < LINE - 1))
            def _():
                back_left_l(t + 1).wait_recv()
                part[t, late] += left_in[t, late].astype(F32)

            left_out[t - 1, late] = part[t, late].astype(BF16)
            back_left_l(t).start()

        @pl.when((t < 4) & (slot(t) <= 2))
        def _():
            @pl.when(t < 3)
            def _():
                back_right_l(t + 1).wait_recv()
                part[ahead, late] += right_in[t, late].astype(F32)

            right_out[t - 1, late] = part[ahead, late].astype(BF16)
            back_right_l(t).start()

        for c in range(2):
            head = pl.ds(2 * c, 2)

            @pl.when(t < 4)
            def _():
                back_right_e(t + 1, c).wait_recv()
                part[ahead, head] += right_in[t, head].astype(F32)

            index = jnp.minimum(2 * t, LINE - 1)
            to_prev(index, c).wait_recv()
            right_out[t - 1, head] = (
                part[ahead, head] + next_part[index, head].astype(F32)
            ).astype(BF16)
            back_right_e(t, c).start()

            @pl.when(t < 4)
            def _():
                @pl.when(t < 3)
                def _():
                    back_left_e(t + 1, c).wait_recv()
                    part[t, head] += left_in[t, head].astype(F32)

                to_prev(2 * t - 1, c).wait_recv()
                left_out[t - 1, head] = (
                    part[t, head] + next_part[2 * t - 1, head].astype(F32)
                ).astype(BF16)
                back_left_e(t, c).start()

    close_rows(0)

    def early_second(i, carry):
        own_second(4 - i, 0)
        return carry

    lax.fori_loop(0, AHEAD, early_second, 0)
    prev_first(4)
    close_rows(2)

    def back_step(i, carry):
        t = 5 - i

        @pl.when(t > 1)
        def _():
            prev_second(t - 1)

        def halves(u, c):
            @pl.when((i > 0) & ((u == 1) | (i > AHEAD)))
            def _():
                own_second(t, 2 * u)

            return c

        lax.fori_loop(0, 2, halves, 0)

        @pl.when((i > 0) & (t > 1))
        def _():
            flush(t)

        return carry

    lax.fori_loop(0, 5, back_step, 0)

    for h in range(KV_HEADS):
        for r in range(SHARE):
            block = dq_t[places[h], :, pl.ds(r * BLOCK, BLOCK)] * SCALE
            dq_ref[:, pl.ds((h * SHARE + r) * BLOCK, BLOCK)] = block.astype(BF16).T
    for c in range(LINE):
        terms[c, :, pl.ds(0, 512)] = dot(
            acts[pl.ds(0, RANK), :], dq_ref[:, pl.ds(c * 512, 512)], 1, 0
        ).astype(BF16)
    for h in range(KV_HEADS):
        terms[h, :, pl.ds(512, BLOCK)] = (kv_terms[2 * places[h]] * SCALE).astype(BF16)
        terms[KV_HEADS + h, :, pl.ds(512, BLOCK)] = kv_terms[2 * places[h] + 1].astype(BF16)

    def stage1_copy(by):
        other = lax.rem(line + by, LINE)
        return copy(
            terms.at[other], stage1.at[by - 1], a_sem1, by - 1, {"ctx": other * LINE + z}
        )

    def stage2_copy(by):
        other = slot(by)
        return copy(
            terms2.at[other // 2], stage2.at[by - 1], a_sem2, by - 1, {"ctx": base + other}
        )

    def stage3_copy(by):
        return copy(terms3, stage3.at[by - 1], a_sem3, by - 1, {"dp": lax.rem(dp + by, 4)})

    for by in range(1, LINE):
        stage1_copy(by).start()
    value = terms[line].astype(F32)
    for by in range(1, LINE):
        stage1_copy(by).wait_recv()
        value = value + stage1[by - 1].astype(F32)
    for c in range(4):
        terms2[c, :, pl.ds(0, BLOCK)] = value[:, c * BLOCK : (c + 1) * BLOCK]
        terms2[c, :, pl.ds(BLOCK, BLOCK)] = value[:, 4 * BLOCK :]
    for by in range(1, LINE):
        stage2_copy(by).start()
    flush(1)
    value = terms2[z // 2]
    for by in range(1, LINE):
        stage2_copy(by).wait_recv()
        value = value + stage2[by - 1]
    terms3[...] = value
    for by in range(1, 4):
        stage3_copy(by).start()

    for c in range(2):
        head = pl.ds(2 * c, 2)
        to_prev(0, c).wait_recv()
        back_left_e(1, c).wait_recv()
        back_right_e(1, c).wait_recv()
        final[head] = (
            part[0, head]
            + next_part[0, head].astype(F32)
            + left_in[0, head].astype(F32)
            + right_in[0, head].astype(F32)
        )
    final[late] = part[0, late]

    @pl.when(z < LINE - 1)
    def _():
        back_left_l(1).wait_recv()
        final[late] += left_in[0, late].astype(F32)

    @pl.when(z <= 2)
    def _():
        back_right_l(1).wait_recv()
        final[late] += right_in[0, late].astype(F32)

    for h in range(KV_HEADS):
        span = pl.ds(h * BLOCK, BLOCK)
        dk_ref[:, span] = (final[2 * places[h]] * SCALE).astype(BF16)
        dv_ref[:, span] = final[2 * places[h] + 1].astype(BF16)

    for by in range(1, 4):
        stage3_copy(by).wait_recv()
        value = value + stage3[by - 1]
    q_first = lax.rem(z, 2) * 64 + dp * 16
    kv_first = z * 16 + dp * 4
    aq_ref[...] = pltpu.roll(value[:, :BLOCK], lax.rem(BLOCK - q_first, BLOCK), 1)[:, :RANK]
    columns[...] = value[:, BLOCK:].T
    akv_ref[...] = columns[pl.ds(kv_first, 4), :]

    for s in range(1, 5):
        for c in range(2):
            left_e(s, c, z).wait_send()
            back_right_e(s, c).wait_send()

        @pl.when((z >= s - 1) & (z < LINE - 1))
        def _():
            right_l(s, z).wait_send()

        @pl.when(z >= s)
        def _():
            back_left_l(s).wait_send()

    for s in range(1, 4):
        for c in range(2):
            right_e(s, c, z).wait_send()
            back_left_e(s, c).wait_send()

        @pl.when(slot(s - 1) <= 2)
        def _():
            left_l(s, z).wait_send()

        @pl.when(slot(s) <= 2)
        def _():
            back_right_l(s).wait_send()

    for index in range(LINE):
        for c in range(2):
            to_next(index, c, z).wait_send()
            to_prev(index, c).wait_send()
    for by in range(1, LINE):
        stage1_copy(by).wait_send()
        stage2_copy(by).wait_send()
    for by in range(1, 4):
        stage3_copy(by).wait_send()


def write_out(*refs):
    count = len(refs) // 2
    for i in range(count):
        refs[count + i][...] = refs[i][...]


def on_device(queries, keys, values, grads_out, ordering, activations):
    count = queries.shape[1]
    vmem = pl.BlockSpec(memory_space=pltpu.VMEM)
    hbm = pl.BlockSpec(memory_space=pltpu.HBM)
    pair = (2 * KV_HEADS, BLOCK, BLOCK)
    half = (KV_HEADS, BLOCK, BLOCK)

    def sems(n):
        return pltpu.SemaphoreType.DMA((2, n))

    shapes = (
        jax.ShapeDtypeStruct((count, queries.shape[2]), BF16),
        jax.ShapeDtypeStruct((count, keys.shape[2]), BF16),
        jax.ShapeDtypeStruct((count, values.shape[2]), BF16),
        jax.ShapeDtypeStruct((RANK, 16), F32),
        jax.ShapeDtypeStruct((4, RANK), F32),
    )
    results = pl.pallas_call(
        kernel,
        out_shape=shapes,
        in_specs=[pl.BlockSpec(memory_space=pltpu.SMEM)] + [hbm] * 5,
        out_specs=(vmem,) * 5,
        scratch_shapes=[
            pltpu.VMEM((KV_HEADS, 2, BLOCK, BLOCK), BF16),
            pltpu.VMEM((LINE, EARLY + HALF, BLOCK), BF16),
            pltpu.VMEM((LINE, EARLY, BLOCK), BF16),
            pltpu.VMEM((KV_HEADS, BLOCK, ROWS), BF16),
            pltpu.VMEM((KV_HEADS, BLOCK, ROWS), BF16),
            pltpu.VMEM((3 * RANK, BLOCK), BF16),
            pltpu.VMEM((KV_HEADS, 1, ROWS), F32),
            pltpu.VMEM((KV_HEADS, 1, ROWS), F32),
            pltpu.VMEM((KV_HEADS, 1, ROWS), F32),
            pltpu.VMEM((2 * BLOCK, ROWS), BF16),
            pltpu.VMEM((2 * BLOCK, ROWS), BF16),
            pltpu.VMEM((KV_HEADS, BLOCK, ROWS), F32),
            pltpu.VMEM((2 * KV_HEADS, RANK, BLOCK), F32),
            pltpu.VMEM((LINE,) + pair, F32),
            pltpu.VMEM((LINE,) + half, BF16),
            pltpu.VMEM((LINE,) + half, BF16),
            pltpu.VMEM((4,) + pair, BF16),
            pltpu.VMEM((4,) + pair, BF16),
            pltpu.VMEM((4,) + pair, BF16),
            pltpu.VMEM((4,) + pair, BF16),
            pltpu.VMEM(pair, F32),
            pltpu.VMEM((LINE, RANK, 5 * BLOCK), BF16),
            pltpu.VMEM((LINE - 1, RANK, 5 * BLOCK), BF16),
            pltpu.VMEM((4, RANK, 2 * BLOCK), F32),
            pltpu.VMEM((LINE - 1, RANK, 2 * BLOCK), F32),
            pltpu.VMEM((RANK, 2 * BLOCK), F32),
            pltpu.VMEM((3, RANK, 2 * BLOCK), F32),
            pltpu.VMEM((BLOCK, RANK), F32),
            sems(KV_HEADS),
            sems(KV_HEADS),
            pltpu.SemaphoreType.DMA((1,)),
            sems(6),
            sems(4),
            sems(8),
            sems(3),
            sems(2 * LINE),
            sems(2 * LINE),
            sems(6),
            sems(4),
            sems(8),
            sems(3),
            sems(LINE - 1),
            sems(LINE - 1),
            sems(3),
        ],
        compiler_params=pltpu.CompilerParams(
            collective_id=0, has_side_effects=True, vmem_limit_bytes=62 << 20
        ),
    )(ordering, queries[0], keys[0], values[0], grads_out[0], activations[0].T)
    dq, dk, dv, aq, akv = pl.pallas_call(
        write_out,
        out_shape=shapes,
        in_specs=[vmem] * 5,
        out_specs=(vmem,) * 5,
        compiler_params=pltpu.CompilerParams(vmem_limit_bytes=62 << 20),
    )(*results)
    return dq[None], dk[None], dv[None], aq, akv.T


def solution(mesh):
    placed = (
        P("dp", "ctx", None),
        P("dp", "ctx", None),
        P("dp", "ctx", None),
        P("dp", "ctx", None),
        P("dp", None),
        P("dp", "ctx", None),
    )
    return jax.shard_map(
        on_device,
        mesh=mesh,
        in_specs=placed,
        out_specs=(
            P("dp", "ctx", None),
            P("dp", "ctx", None),
            P("dp", "ctx", None),
            P(None, ("ctx", "dp")),
            P(None, ("ctx", "dp")),
        ),
        check_vma=False,
    )
```

```python
import math

import jax
import jax.numpy as jnp
from jax import lax
from jax.experimental import pallas as pl
from jax.experimental.pallas import tpu as pltpu
from jax.sharding import PartitionSpec as P

MESH = pl.DeviceIdType.MESH
F32 = jnp.float32
BF16 = jnp.bfloat16
BLOCK = 128
KV_HEADS = 4
SHARE = 8
ROWS = SHARE * BLOCK
AHEAD = 1
LINE = 8
RANK = 16
SCALE = 1.0 / math.sqrt(BLOCK)
EXP2_SCALE = SCALE / math.log(2.0)
HIDDEN = -1e30
ACT = 2 * RANK
HALF = 4 * BLOCK
EARLY = ACT + HALF
CHUNKS = ((0, ACT + 2 * BLOCK), (ACT + 2 * BLOCK, 2 * BLOCK))


def dot(a, b, a_dim, b_dim):
    return lax.dot_general(a, b, (((a_dim,), (b_dim,)), ((), ())), preferred_element_type=F32)


def kernel(
    order_ref,
    q_ref,
    k_ref,
    v_ref,
    g_ref,
    act_ref,
    dq_ref,
    dk_ref,
    dv_ref,
    aq_ref,
    akv_ref,
    own_kv,
    line_kv,
    prev_kv,
    qs,
    gs,
    acts,
    top,
    total,
    accum,
    p_low,
    s_low,
    dq_t,
    kv_terms,
    part,
    prev_part,
    next_part,
    left_out,
    left_in,
    right_out,
    right_in,
    final,
    terms,
    stage1,
    terms2,
    stage2,
    terms3,
    stage3,
    columns,
    load_sem,
    kv_sem,
    act_sem,
    g_right_e,
    g_right_l,
    g_left_e,
    g_left_l,
    g_next,
    b_prev,
    b_left_e,
    b_left_l,
    b_right_e,
    b_right_l,
    a_sem1,
    a_sem2,
    a_sem3,
):
    ctx = lax.axis_index("ctx")
    dp = lax.axis_index("dp")
    z = lax.rem(ctx, LINE)
    line = ctx // LINE
    base = line * LINE
    left = base + lax.rem(z + LINE - 1, LINE)
    right = base + lax.rem(z + 1, LINE)
    after = lax.rem(line + 1, LINE) * LINE + z
    before = lax.rem(line + LINE - 1, LINE) * LINE + z

    def copy(src, dst, sems, index, target):
        return pltpu.make_async_remote_copy(
            src_ref=src,
            dst_ref=dst,
            send_sem=sems.at[0, index],
            recv_sem=sems.at[1, index],
            device_id=target,
            device_id_type=MESH,
        )

    def slot(by):
        return lax.rem(z + by + LINE, LINE)

    def right_e(s, c, block):
        view = line_kv.at[block, pl.ds(*CHUNKS[c])]
        return copy(view, view, g_right_e, 2 * (s - 1) + c, {"ctx": right})

    def right_l(s, block):
        view = line_kv.at[block, pl.ds(EARLY, HALF)]
        return copy(view, view, g_right_l, s - 1, {"ctx": right})

    def left_e(s, c, block):
        view = line_kv.at[block, pl.ds(*CHUNKS[c])]
        return copy(view, view, g_left_e, 2 * (s - 1) + c, {"ctx": left})

    def left_l(s, block):
        view = line_kv.at[block, pl.ds(EARLY, HALF)]
        return copy(view, view, g_left_l, s - 1, {"ctx": left})

    def to_next(index, c, block):
        rows = pl.ds(*CHUNKS[c])
        return copy(
            line_kv.at[block, rows],
            prev_kv.at[block, rows],
            g_next,
            2 * index + c,
            {"ctx": after},
        )

    def to_prev(index, c):
        view = pl.ds(2 * c, 2)
        return copy(
            prev_part.at[index, view],
            next_part.at[index, view],
            b_prev,
            2 * index + c,
            {"ctx": before},
        )

    def back_left_e(s, c):
        view = pl.ds(2 * c, 2)
        return copy(
            left_out.at[s - 1, view],
            left_in.at[s - 1, view],
            b_left_e,
            2 * (s - 1) + c,
            {"ctx": left},
        )

    def back_right_e(s, c):
        view = pl.ds(2 * c, 2)
        return copy(
            right_out.at[s - 1, view],
            right_in.at[s - 1, view],
            b_right_e,
            2 * (s - 1) + c,
            {"ctx": right},
        )

    def back_left_l(s):
        return copy(
            left_out.at[s - 1, pl.ds(4, 4)],
            left_in.at[s - 1, pl.ds(4, 4)],
            b_left_l,
            s - 1,
            {"ctx": left},
        )

    def back_right_l(s):
        return copy(
            right_out.at[s - 1, pl.ds(4, 4)],
            right_in.at[s - 1, pl.ds(4, 4)],
            b_right_l,
            s - 1,
            {"ctx": right},
        )

    def load(src, dst, row, h):
        return pltpu.make_async_copy(
            src.at[:, pl.ds(h * ROWS, ROWS)], dst.at[h], load_sem.at[row, h]
        )

    def load_kv(src, which, h):
        return pltpu.make_async_copy(
            src.at[:, pl.ds(h * BLOCK, BLOCK)], own_kv.at[h, which], kv_sem.at[which, h]
        )

    barrier = pltpu.get_barrier_semaphore()
    for by in range(1, LINE):
        pl.semaphore_signal(barrier, inc=1, device_id={"ctx": base + slot(by)}, device_id_type=MESH)
        pl.semaphore_signal(
            barrier,
            inc=1,
            device_id={"ctx": lax.rem(line + by, LINE) * LINE + z},
            device_id_type=MESH,
        )
    for by in range(1, 4):
        pl.semaphore_signal(
            barrier, inc=1, device_id={"dp": lax.rem(dp + by, 4)}, device_id_type=MESH
        )

    load_act = pltpu.make_async_copy(act_ref, acts, act_sem.at[0])
    for h in range(KV_HEADS):
        load_kv(k_ref, 0, h).start()
        load_kv(v_ref, 1, h).start()
    load_act.start()

    swap = 2 * (1 - lax.rem(line, 2))
    ordering = [order_ref[0, lax.rem(j + swap, KV_HEADS)] for j in range(KV_HEADS)]
    places = []
    for h in range(KV_HEADS):
        place = jnp.int32(0)
        for j in range(1, KV_HEADS):
            place = jnp.maximum(place, jnp.where(ordering[j] == h, j, 0))
        places.append(place)

    for h in range(KV_HEADS):
        load_kv(k_ref, 0, h).wait()
        load_kv(v_ref, 1, h).wait()
    load_act.wait()
    line_kv[z, pl.ds(0, ACT), :] = acts[pl.ds(RANK, ACT), :]
    for j in range(KV_HEADS):
        first = ACT + 2 * j * BLOCK
        line_kv[z, pl.ds(first, BLOCK), :] = own_kv[ordering[j], 0]
        line_kv[z, pl.ds(first + BLOCK, BLOCK), :] = own_kv[ordering[j], 1]

    pl.semaphore_wait(barrier, 2 * (LINE - 1) + 3)
    for c in range(2):
        left_e(1, c, z).start()
        right_e(1, c, z).start()
        to_next(0, c, z).start()

    for h in range(KV_HEADS):
        load(q_ref, qs, 0, h).start()
        load(g_ref, gs, 1, h).start()

    width = 2 * BLOCK

    def name(j):
        return order_ref[0, lax.rem(j + swap, KV_HEADS)]

    def rows_of(source, j, first, count):
        heads = [source[name(j), :, pl.ds(r * BLOCK, BLOCK)] for r in range(first, first + count)]
        return jnp.concatenate(heads, axis=0)

    def scores(j, piece, keys, diagonal):
        q = rows_of(qs, j, 2 * piece, 2)
        s = dot(keys, q, 1, 1) * EXP2_SCALE
        if diagonal:
            key_at = lax.broadcasted_iota(jnp.int32, (BLOCK, width), 0)
            query_at = lax.rem(lax.broadcasted_iota(jnp.int32, (BLOCK, width), 1), BLOCK)
            own = jnp.where(key_at <= query_at, s[-BLOCK:], HIDDEN)
            s = own if s.shape[0] == BLOCK else jnp.concatenate([s[:-BLOCK], own], axis=0)
        return s

    def first_pass(j, keys, values, diagonal):
        for piece in range(ROWS // width):
            cols = pl.ds(piece * width, width)
            s = scores(j, piece, keys, diagonal)
            old = top[j, :, cols]
            new = jnp.maximum(old, jnp.max(s, axis=0, keepdims=True))
            e = jnp.exp2(s - new)
            dp_ = dot(values, rows_of(gs, j, 2 * piece, 2), 1, 1)
            factor = jnp.exp2(old - new)
            total[j, :, cols] = total[j, :, cols] * factor + jnp.sum(e, axis=0, keepdims=True)
            accum[j, :, cols] = accum[j, :, cols] * factor + jnp.sum(e * dp_, axis=0, keepdims=True)
            top[j, :, cols] = new

    def second_pass(j, keys, values, acts_k, acts_v, diagonal):
        count = keys.shape[0]
        for piece in range(ROWS // width):
            cols = pl.ds(piece * width, width)
            p = jnp.exp2(scores(j, piece, keys, diagonal) - top[j, :, cols])
            dp_ = dot(values, rows_of(gs, j, 2 * piece, 2), 1, 1)
            s_low[pl.ds(0, count), cols] = (p * (dp_ - accum[j, :, cols])).astype(BF16)
            p_low[pl.ds(0, count), cols] = p.astype(BF16)
        ds = s_low[pl.ds(0, count), :]
        dk = dot(ds, rows_of(qs, j, 0, SHARE), 1, 0)
        dv = dot(p_low[pl.ds(0, count), :], rows_of(gs, j, 0, SHARE), 1, 0)
        dq_t[j] += dot(keys, ds, 0, 0)
        kv_terms[2 * j] += dot(acts_k, dk.astype(BF16), 1, 0)
        kv_terms[2 * j + 1] += dot(acts_v, dv.astype(BF16), 1, 0)
        return dk, dv

    def keys_of(source, j, blocks):
        first = pl.multiple_of(ACT + 2 * j * BLOCK, ACT)
        keys = [source[b, pl.ds(first, BLOCK), :] for b in blocks]
        values = [source[b, pl.ds(first + BLOCK, BLOCK), :] for b in blocks]
        if len(blocks) == 1:
            return keys[0], values[0]
        return jnp.concatenate(keys, axis=0), jnp.concatenate(values, axis=0)

    def acts_of(source, blocks):
        sides = [source[b, pl.ds(0, ACT), :] for b in blocks]
        both = sides[0] if len(blocks) == 1 else jnp.concatenate(sides, axis=1)
        return both[:RANK], both[RANK:]

    def own_cases(t, run):
        far = 9 - t

        @pl.when((t == 1) & (z >= 1))
        def _():
            run((1, 0), True)

        @pl.when((t == 1) & (z == 0))
        def _():
            run((0,), True)

        @pl.when((t > 1) & (z >= far))
        def _():
            run((t, far), False)

        @pl.when((t > 1) & (z >= t) & (z < far))
        def _():
            run((t,), False)

    def prev_pair(t):
        second = jnp.where(t == 1, 0, 2 * t - 2)
        return (2 * t - 1, second), (slot(-t), lax.rem(z + t - 1, LINE))

    def own_first(t, first):
        def run(distances, diagonal):
            blocks = [slot(-d) for d in distances]

            def head(j, c):
                keys, values = keys_of(line_kv, j, blocks)
                first_pass(j, keys, values, diagonal)
                return c

            lax.fori_loop(first, first + 2, head, 0)

        own_cases(t, run)

    def prev_first(t):
        indices, blocks = prev_pair(t)
        for index, b in zip(indices, blocks):
            for c in range(2):
                to_next(index, c, b).wait_recv()

        def head(j, c):
            keys, values = keys_of(prev_kv, j, blocks)
            first_pass(j + 2, keys, values, False)
            return c

        lax.fori_loop(0, 2, head, 0)

    def early_step(t):
        block = slot(-t)
        other = slot(t)
        for c in range(2):
            left_e(t, c, other).wait_recv()

            @pl.when(t < 4)
            def _():
                left_e(t + 1, c, other).start()

            to_next(jnp.minimum(2 * t, LINE - 1), c, other).start()

            @pl.when(t < 4)
            def _():
                right_e(t, c, block).wait_recv()

                @pl.when(t < 3)
                def _():
                    right_e(t + 1, c, block).start()

                to_next(2 * t - 1, c, block).start()

    def late_step(t):
        @pl.when(z >= t)
        def _():
            @pl.when(t > 0)
            def _():
                right_l(t, slot(-t)).wait_recv()

            @pl.when((t < 4) & (z < LINE - 1))
            def _():
                right_l(t + 1, slot(-t)).start()

        @pl.when((t < 4) & (slot(t) <= 2))
        def _():
            @pl.when(t > 0)
            def _():
                left_l(t, slot(t)).wait_recv()

            @pl.when(t < 3)
            def _():
                left_l(t + 1, slot(t)).start()

    def begin():
        top[...] = jnp.full(top.shape, HIDDEN, F32)
        total[...] = jnp.zeros(total.shape, F32)
        accum[...] = jnp.zeros(accum.shape, F32)
        dq_t[...] = jnp.zeros(dq_t.shape, F32)
        kv_terms[...] = jnp.zeros(kv_terms.shape, F32)
        for d in range(LINE):
            part[d] = jnp.zeros(part.shape[1:], F32)
        for h in range(KV_HEADS):
            load(q_ref, qs, 0, h).wait()
            load(g_ref, gs, 1, h).wait()

    def gather_step(t, carry):
        early_step(t)

        @pl.when(t == 1)
        def _():
            begin()

        def halves(u, c):
            @pl.when(u == 1)
            def _():
                late_step(t)

            own_first(t, 2 * u)
            return c

        lax.fori_loop(0, 2, halves, 0)

        @pl.when(t > 1)
        def _():
            prev_first(t - 1)

        return carry

    late_step(0)
    lax.fori_loop(1, 5, gather_step, 0)

    def close_rows(first):
        heads = pl.ds(first, 2)
        top[heads] = top[heads] + jnp.log2(total[heads])
        accum[heads] = accum[heads] / total[heads]

    def own_second(t, first):
        def run(distances, diagonal):
            blocks = [slot(-d) for d in distances]
            acts_k, acts_v = acts_of(line_kv, blocks)

            def head(j, c):
                keys, values = keys_of(line_kv, j, blocks)
                dk, dv = second_pass(j, keys, values, acts_k, acts_v, diagonal)
                for i, d in enumerate(distances):
                    rows = slice(i * BLOCK, (i + 1) * BLOCK)
                    part[d, 2 * j] = dk[rows]
                    part[d, 2 * j + 1] = dv[rows]
                return c

            lax.fori_loop(first, first + 2, head, 0)

        own_cases(t, run)

    def prev_second(t):
        indices, blocks = prev_pair(t)
        acts_k, acts_v = acts_of(prev_kv, blocks)

        def head(j, c):
            keys, values = keys_of(prev_kv, j, blocks)
            dk, dv = second_pass(j + 2, keys, values, acts_k, acts_v, False)
            for i, index in enumerate(indices):
                rows = slice(i * BLOCK, (i + 1) * BLOCK)
                prev_part[index, 2 * j] = dk[rows].astype(BF16)
                prev_part[index, 2 * j + 1] = dv[rows].astype(BF16)
            return c

        lax.fori_loop(0, 2, head, 0)
        for index in indices:
            for c in range(2):
                to_prev(index, c).start()

    late = pl.ds(4, 4)

    def flush(t):
        ahead = LINE - t

        @pl.when(z >= t)
        def _():
            @pl.when((t < 4) & (z < LINE - 1))
            def _():
                back_left_l(t + 1).wait_recv()
                part[t, late] += left_in[t, late].astype(F32)

            left_out[t - 1, late] = part[t, late].astype(BF16)
            back_left_l(t).start()

        @pl.when((t < 4) & (slot(t) <= 2))
        def _():
            @pl.when(t < 3)
            def _():
                back_right_l(t + 1).wait_recv()
                part[ahead, late] += right_in[t, late].astype(F32)

            right_out[t - 1, late] = part[ahead, late].astype(BF16)
            back_right_l(t).start()

        for c in range(2):
            head = pl.ds(2 * c, 2)

            @pl.when(t < 4)
            def _():
                back_right_e(t + 1, c).wait_recv()
                part[ahead, head] += right_in[t, head].astype(F32)

            index = jnp.minimum(2 * t, LINE - 1)
            to_prev(index, c).wait_recv()
            right_out[t - 1, head] = (
                part[ahead, head] + next_part[index, head].astype(F32)
            ).astype(BF16)
            back_right_e(t, c).start()

            @pl.when(t < 4)
            def _():
                @pl.when(t < 3)
                def _():
                    back_left_e(t + 1, c).wait_recv()
                    part[t, head] += left_in[t, head].astype(F32)

                to_prev(2 * t - 1, c).wait_recv()
                left_out[t - 1, head] = (
                    part[t, head] + next_part[2 * t - 1, head].astype(F32)
                ).astype(BF16)
                back_left_e(t, c).start()

    close_rows(0)

    def early_second(i, carry):
        own_second(4 - i, 0)
        return carry

    lax.fori_loop(0, AHEAD, early_second, 0)
    prev_first(4)
    close_rows(2)

    def back_step(i, carry):
        t = 5 - i

        @pl.when(t > 1)
        def _():
            prev_second(t - 1)

        @pl.when((i > 1) & (t > 1))
        def _():
            flush(t + 1)

        def halves(u, c):
            @pl.when((i > 0) & ((u == 1) | (i > AHEAD)))
            def _():
                own_second(t, 2 * u)

            return c

        lax.fori_loop(0, 2, halves, 0)

        return carry

    lax.fori_loop(0, 5, back_step, 0)

    def low_block(h, r):
        return (dq_t[places[h], :, pl.ds(r * BLOCK, BLOCK)] * SCALE).astype(BF16)

    for h in range(KV_HEADS):
        for r in range(SHARE):
            term = dot(acts[pl.ds(0, RANK), :], low_block(h, r), 1, 1).astype(BF16)
            c, column = divmod(h * SHARE + r, 4)
            terms[c, :, pl.ds(column * BLOCK, BLOCK)] = term
    for h in range(KV_HEADS):
        terms[h, :, pl.ds(512, BLOCK)] = (kv_terms[2 * places[h]] * SCALE).astype(BF16)
        terms[KV_HEADS + h, :, pl.ds(512, BLOCK)] = kv_terms[2 * places[h] + 1].astype(BF16)

    def stage1_copy(by):
        other = lax.rem(line + by, LINE)
        return copy(
            terms.at[other], stage1.at[by - 1], a_sem1, by - 1, {"ctx": other * LINE + z}
        )

    def stage2_copy(by):
        other = slot(by)
        return copy(
            terms2.at[other // 2], stage2.at[by - 1], a_sem2, by - 1, {"ctx": base + other}
        )

    def stage3_copy(by):
        return copy(terms3, stage3.at[by - 1], a_sem3, by - 1, {"dp": lax.rem(dp + by, 4)})

    for by in range(1, LINE):
        stage1_copy(by).start()
    for h in range(KV_HEADS):
        for r in range(SHARE):
            dq_ref[:, pl.ds((h * SHARE + r) * BLOCK, BLOCK)] = low_block(h, r).T
    flush(2)
    value = terms[line].astype(F32)
    for by in range(1, LINE):
        stage1_copy(by).wait_recv()
        value = value + stage1[by - 1].astype(F32)
    for c in range(4):
        terms2[c, :, pl.ds(0, BLOCK)] = value[:, c * BLOCK : (c + 1) * BLOCK]
        terms2[c, :, pl.ds(BLOCK, BLOCK)] = value[:, 4 * BLOCK :]
    for by in range(1, LINE):
        stage2_copy(by).start()
    flush(1)
    value = terms2[z // 2]
    for by in range(1, LINE):
        stage2_copy(by).wait_recv()
        value = value + stage2[by - 1]
    terms3[...] = value
    for by in range(1, 4):
        stage3_copy(by).start()

    for c in range(2):
        head = pl.ds(2 * c, 2)
        to_prev(0, c).wait_recv()
        back_left_e(1, c).wait_recv()
        back_right_e(1, c).wait_recv()
        final[head] = (
            part[0, head]
            + next_part[0, head].astype(F32)
            + left_in[0, head].astype(F32)
            + right_in[0, head].astype(F32)
        )
    final[late] = part[0, late]

    @pl.when(z < LINE - 1)
    def _():
        back_left_l(1).wait_recv()
        final[late] += left_in[0, late].astype(F32)

    @pl.when(z <= 2)
    def _():
        back_right_l(1).wait_recv()
        final[late] += right_in[0, late].astype(F32)

    for h in range(KV_HEADS):
        span = pl.ds(h * BLOCK, BLOCK)
        dk_ref[:, span] = (final[2 * places[h]] * SCALE).astype(BF16)
        dv_ref[:, span] = final[2 * places[h] + 1].astype(BF16)

    for by in range(1, 4):
        stage3_copy(by).wait_recv()
        value = value + stage3[by - 1]
    q_first = lax.rem(z, 2) * 64 + dp * 16
    kv_first = z * 16 + dp * 4
    aq_ref[...] = pltpu.roll(value[:, :BLOCK], lax.rem(BLOCK - q_first, BLOCK), 1)[:, :RANK]
    columns[...] = value[:, BLOCK:].T
    akv_ref[...] = columns[pl.ds(kv_first, 4), :]

    for s in range(1, 5):
        for c in range(2):
            left_e(s, c, z).wait_send()
            back_right_e(s, c).wait_send()

        @pl.when((z >= s - 1) & (z < LINE - 1))
        def _():
            right_l(s, z).wait_send()

        @pl.when(z >= s)
        def _():
            back_left_l(s).wait_send()

    for s in range(1, 4):
        for c in range(2):
            right_e(s, c, z).wait_send()
            back_left_e(s, c).wait_send()

        @pl.when(slot(s - 1) <= 2)
        def _():
            left_l(s, z).wait_send()

        @pl.when(slot(s) <= 2)
        def _():
            back_right_l(s).wait_send()

    for index in range(LINE):
        for c in range(2):
            to_next(index, c, z).wait_send()
            to_prev(index, c).wait_send()
    for by in range(1, LINE):
        stage1_copy(by).wait_send()
        stage2_copy(by).wait_send()
    for by in range(1, 4):
        stage3_copy(by).wait_send()


def write_out(*refs):
    count = len(refs) // 2
    for i in range(count):
        refs[count + i][...] = refs[i][...]


def on_device(queries, keys, values, grads_out, ordering, activations):
    count = queries.shape[1]
    vmem = pl.BlockSpec(memory_space=pltpu.VMEM)
    hbm = pl.BlockSpec(memory_space=pltpu.HBM)
    pair = (2 * KV_HEADS, BLOCK, BLOCK)
    half = (KV_HEADS, BLOCK, BLOCK)

    def sems(n):
        return pltpu.SemaphoreType.DMA((2, n))

    shapes = (
        jax.ShapeDtypeStruct((count, queries.shape[2]), BF16),
        jax.ShapeDtypeStruct((count, keys.shape[2]), BF16),
        jax.ShapeDtypeStruct((count, values.shape[2]), BF16),
        jax.ShapeDtypeStruct((RANK, 16), F32),
        jax.ShapeDtypeStruct((4, RANK), F32),
    )
    results = pl.pallas_call(
        kernel,
        out_shape=shapes,
        in_specs=[pl.BlockSpec(memory_space=pltpu.SMEM)] + [hbm] * 5,
        out_specs=(vmem,) * 5,
        scratch_shapes=[
            pltpu.VMEM((KV_HEADS, 2, BLOCK, BLOCK), BF16),
            pltpu.VMEM((LINE, EARLY + HALF, BLOCK), BF16),
            pltpu.VMEM((LINE, EARLY, BLOCK), BF16),
            pltpu.VMEM((KV_HEADS, BLOCK, ROWS), BF16),
            pltpu.VMEM((KV_HEADS, BLOCK, ROWS), BF16),
            pltpu.VMEM((3 * RANK, BLOCK), BF16),
            pltpu.VMEM((KV_HEADS, 1, ROWS), F32),
            pltpu.VMEM((KV_HEADS, 1, ROWS), F32),
            pltpu.VMEM((KV_HEADS, 1, ROWS), F32),
            pltpu.VMEM((2 * BLOCK, ROWS), BF16),
            pltpu.VMEM((2 * BLOCK, ROWS), BF16),
            pltpu.VMEM((KV_HEADS, BLOCK, ROWS), F32),
            pltpu.VMEM((2 * KV_HEADS, RANK, BLOCK), F32),
            pltpu.VMEM((LINE,) + pair, F32),
            pltpu.VMEM((LINE,) + half, BF16),
            pltpu.VMEM((LINE,) + half, BF16),
            pltpu.VMEM((4,) + pair, BF16),
            pltpu.VMEM((4,) + pair, BF16),
            pltpu.VMEM((4,) + pair, BF16),
            pltpu.VMEM((4,) + pair, BF16),
            pltpu.VMEM(pair, F32),
            pltpu.VMEM((LINE, RANK, 5 * BLOCK), BF16),
            pltpu.VMEM((LINE - 1, RANK, 5 * BLOCK), BF16),
            pltpu.VMEM((4, RANK, 2 * BLOCK), F32),
            pltpu.VMEM((LINE - 1, RANK, 2 * BLOCK), F32),
            pltpu.VMEM((RANK, 2 * BLOCK), F32),
            pltpu.VMEM((3, RANK, 2 * BLOCK), F32),
            pltpu.VMEM((BLOCK, RANK), F32),
            sems(KV_HEADS),
            sems(KV_HEADS),
            pltpu.SemaphoreType.DMA((1,)),
            sems(6),
            sems(4),
            sems(8),
            sems(3),
            sems(2 * LINE),
            sems(2 * LINE),
            sems(6),
            sems(4),
            sems(8),
            sems(3),
            sems(LINE - 1),
            sems(LINE - 1),
            sems(3),
        ],
        compiler_params=pltpu.CompilerParams(
            collective_id=0, has_side_effects=True, vmem_limit_bytes=62 << 20
        ),
    )(ordering, queries[0], keys[0], values[0], grads_out[0], activations[0].T)
    dq, dk, dv, aq, akv = pl.pallas_call(
        write_out,
        out_shape=shapes,
        in_specs=[vmem] * 5,
        out_specs=(vmem,) * 5,
        compiler_params=pltpu.CompilerParams(vmem_limit_bytes=62 << 20),
    )(*results)
    return dq[None], dk[None], dv[None], aq, akv.T


def solution(mesh):
    placed = (
        P("dp", "ctx", None),
        P("dp", "ctx", None),
        P("dp", "ctx", None),
        P("dp", "ctx", None),
        P("dp", None),
        P("dp", "ctx", None),
    )
    return jax.shard_map(
        on_device,
        mesh=mesh,
        in_specs=placed,
        out_specs=(
            P("dp", "ctx", None),
            P("dp", "ctx", None),
            P("dp", "ctx", None),
            P(None, ("ctx", "dp")),
            P(None, ("ctx", "dp")),
        ),
        check_vma=False,
    )
```

```python
import math

import jax
import jax.numpy as jnp
from jax import lax
from jax.experimental import pallas as pl
from jax.experimental.pallas import tpu as pltpu
from jax.sharding import PartitionSpec as P

MESH = pl.DeviceIdType.MESH
F32 = jnp.float32
BF16 = jnp.bfloat16
BLOCK = 128
KV_HEADS = 4
SHARE = 8
ROWS = SHARE * BLOCK
AHEAD = 1
LINE = 8
RANK = 16
SCALE = 1.0 / math.sqrt(BLOCK)
EXP2_SCALE = SCALE / math.log(2.0)
HIDDEN = -1e30
ACT = 2 * RANK
HALF = 4 * BLOCK
EARLY = ACT + HALF
CHUNKS = ((0, ACT + 2 * BLOCK), (ACT + 2 * BLOCK, 2 * BLOCK))


def dot(a, b, a_dim, b_dim):
    return lax.dot_general(a, b, (((a_dim,), (b_dim,)), ((), ())), preferred_element_type=F32)


def kernel(
    order_ref,
    q_ref,
    k_ref,
    v_ref,
    g_ref,
    act_ref,
    dq_ref,
    dk_ref,
    dv_ref,
    aq_ref,
    akv_ref,
    own_kv,
    line_kv,
    prev_kv,
    qs,
    gs,
    acts,
    top,
    total,
    accum,
    p_low,
    s_low,
    dq_t,
    kv_terms,
    part,
    prev_part,
    side_in,
    next_part,
    left_out,
    left_in,
    right_out,
    right_in,
    final,
    terms,
    stage1,
    terms2,
    stage2,
    terms3,
    stage3,
    columns,
    load_sem,
    kv_sem,
    act_sem,
    g_right_e,
    g_right_l,
    g_left_e,
    g_left_l,
    g_next,
    g_side,
    b_side,
    b_prev,
    b_left_e,
    b_left_l,
    b_right_e,
    b_right_l,
    a_sem1,
    a_sem2,
    a_sem3,
):
    ctx = lax.axis_index("ctx")
    dp = lax.axis_index("dp")
    z = lax.rem(ctx, LINE)
    line = ctx // LINE
    base = line * LINE
    left = base + lax.rem(z + LINE - 1, LINE)
    right = base + lax.rem(z + 1, LINE)
    after = lax.rem(line + 1, LINE) * LINE + z
    before = lax.rem(line + LINE - 1, LINE) * LINE + z

    def copy(src, dst, sems, index, target):
        return pltpu.make_async_remote_copy(
            src_ref=src,
            dst_ref=dst,
            send_sem=sems.at[0, index],
            recv_sem=sems.at[1, index],
            device_id=target,
            device_id_type=MESH,
        )

    def slot(by):
        return lax.rem(z + by + LINE, LINE)

    def right_e(s, c, block):
        view = line_kv.at[block, pl.ds(*CHUNKS[c])]
        return copy(view, view, g_right_e, 2 * (s - 1) + c, {"ctx": right})

    def right_l(s, block):
        view = line_kv.at[block, pl.ds(EARLY, HALF)]
        return copy(view, view, g_right_l, s - 1, {"ctx": right})

    def left_e(s, c, block):
        view = line_kv.at[block, pl.ds(*CHUNKS[c])]
        return copy(view, view, g_left_e, 2 * (s - 1) + c, {"ctx": left})

    def left_l(s, block):
        view = line_kv.at[block, pl.ds(EARLY, HALF)]
        return copy(view, view, g_left_l, s - 1, {"ctx": left})

    def to_next(index, c, block):
        rows = pl.ds(*CHUNKS[c])
        return copy(
            line_kv.at[block, rows],
            prev_kv.at[block, rows],
            g_next,
            2 * index + c,
            {"ctx": after},
        )

    def side_right(block):
        view = prev_kv.at[block, pl.ds(*CHUNKS[0])]
        return copy(view, view, g_side, 0, {"ctx": right})

    def side_left(block):
        view = prev_kv.at[block, pl.ds(*CHUNKS[1])]
        return copy(view, view, g_side, 1, {"ctx": left})

    def side_back(c):
        index, target = ((3, left), (4, right))[c]
        return copy(
            prev_part.at[index, pl.ds(2 * c, 2)], side_in.at[c], b_side, c, {"ctx": target}
        )

    def to_prev(index, c):
        view = pl.ds(2 * c, 2)
        return copy(
            prev_part.at[index, view],
            next_part.at[index, view],
            b_prev,
            2 * index + c,
            {"ctx": before},
        )

    def back_left_e(s, c):
        view = pl.ds(2 * c, 2)
        return copy(
            left_out.at[s - 1, view],
            left_in.at[s - 1, view],
            b_left_e,
            2 * (s - 1) + c,
            {"ctx": left},
        )

    def back_right_e(s, c):
        view = pl.ds(2 * c, 2)
        return copy(
            right_out.at[s - 1, view],
            right_in.at[s - 1, view],
            b_right_e,
            2 * (s - 1) + c,
            {"ctx": right},
        )

    def back_left_l(s):
        return copy(
            left_out.at[s - 1, pl.ds(4, 4)],
            left_in.at[s - 1, pl.ds(4, 4)],
            b_left_l,
            s - 1,
            {"ctx": left},
        )

    def back_right_l(s):
        return copy(
            right_out.at[s - 1, pl.ds(4, 4)],
            right_in.at[s - 1, pl.ds(4, 4)],
            b_right_l,
            s - 1,
            {"ctx": right},
        )

    def load(src, dst, row, h):
        return pltpu.make_async_copy(
            src.at[:, pl.ds(h * ROWS, ROWS)], dst.at[h], load_sem.at[row, h]
        )

    def load_kv(src, which, h):
        return pltpu.make_async_copy(
            src.at[:, pl.ds(h * BLOCK, BLOCK)], own_kv.at[h, which], kv_sem.at[which, h]
        )

    barrier = pltpu.get_barrier_semaphore()
    for by in range(1, LINE):
        pl.semaphore_signal(barrier, inc=1, device_id={"ctx": base + slot(by)}, device_id_type=MESH)
        pl.semaphore_signal(
            barrier,
            inc=1,
            device_id={"ctx": lax.rem(line + by, LINE) * LINE + z},
            device_id_type=MESH,
        )
    for by in range(1, 4):
        pl.semaphore_signal(
            barrier, inc=1, device_id={"dp": lax.rem(dp + by, 4)}, device_id_type=MESH
        )

    load_act = pltpu.make_async_copy(act_ref, acts, act_sem.at[0])
    for h in range(KV_HEADS):
        load_kv(k_ref, 0, h).start()
        load_kv(v_ref, 1, h).start()
    load_act.start()

    swap = 2 * (1 - lax.rem(line, 2))
    ordering = [order_ref[0, lax.rem(j + swap, KV_HEADS)] for j in range(KV_HEADS)]
    places = []
    for h in range(KV_HEADS):
        place = jnp.int32(0)
        for j in range(1, KV_HEADS):
            place = jnp.maximum(place, jnp.where(ordering[j] == h, j, 0))
        places.append(place)

    for h in range(KV_HEADS):
        load_kv(k_ref, 0, h).wait()
        load_kv(v_ref, 1, h).wait()
    load_act.wait()
    line_kv[z, pl.ds(0, ACT), :] = acts[pl.ds(RANK, ACT), :]
    for j in range(KV_HEADS):
        first = ACT + 2 * j * BLOCK
        line_kv[z, pl.ds(first, BLOCK), :] = own_kv[ordering[j], 0]
        line_kv[z, pl.ds(first + BLOCK, BLOCK), :] = own_kv[ordering[j], 1]

    pl.semaphore_wait(barrier, 2 * (LINE - 1) + 3)
    for c in range(2):
        left_e(1, c, z).start()
        right_e(1, c, z).start()
        to_next(0, c, z).start()

    for h in range(KV_HEADS):
        load(q_ref, qs, 0, h).start()
        load(g_ref, gs, 1, h).start()

    width = 2 * BLOCK

    def name(j):
        return order_ref[0, lax.rem(j + swap, KV_HEADS)]

    def rows_of(source, j, first, count):
        heads = [source[name(j), :, pl.ds(r * BLOCK, BLOCK)] for r in range(first, first + count)]
        return jnp.concatenate(heads, axis=0)

    def scores(j, piece, keys, diagonal):
        q = rows_of(qs, j, 2 * piece, 2)
        s = dot(keys, q, 1, 1) * EXP2_SCALE
        if diagonal:
            key_at = lax.broadcasted_iota(jnp.int32, (BLOCK, width), 0)
            query_at = lax.rem(lax.broadcasted_iota(jnp.int32, (BLOCK, width), 1), BLOCK)
            own = jnp.where(key_at <= query_at, s[-BLOCK:], HIDDEN)
            s = own if s.shape[0] == BLOCK else jnp.concatenate([s[:-BLOCK], own], axis=0)
        return s

    def first_pass(j, keys, values, diagonal):
        for piece in range(ROWS // width):
            cols = pl.ds(piece * width, width)
            s = scores(j, piece, keys, diagonal)
            old = top[j, :, cols]
            new = jnp.maximum(old, jnp.max(s, axis=0, keepdims=True))
            e = jnp.exp2(s - new)
            dp_ = dot(values, rows_of(gs, j, 2 * piece, 2), 1, 1)
            factor = jnp.exp2(old - new)
            total[j, :, cols] = total[j, :, cols] * factor + jnp.sum(e, axis=0, keepdims=True)
            accum[j, :, cols] = accum[j, :, cols] * factor + jnp.sum(e * dp_, axis=0, keepdims=True)
            top[j, :, cols] = new

    def second_pass(j, keys, values, acts_k, acts_v, diagonal):
        count = keys.shape[0]
        for piece in range(ROWS // width):
            cols = pl.ds(piece * width, width)
            p = jnp.exp2(scores(j, piece, keys, diagonal) - top[j, :, cols])
            dp_ = dot(values, rows_of(gs, j, 2 * piece, 2), 1, 1)
            s_low[pl.ds(0, count), cols] = (p * (dp_ - accum[j, :, cols])).astype(BF16)
            p_low[pl.ds(0, count), cols] = p.astype(BF16)
        ds = s_low[pl.ds(0, count), :]
        dk = dot(ds, rows_of(qs, j, 0, SHARE), 1, 0)
        dv = dot(p_low[pl.ds(0, count), :], rows_of(gs, j, 0, SHARE), 1, 0)
        dq_t[j] += dot(keys, ds, 0, 0)
        kv_terms[2 * j] += dot(acts_k, dk.astype(BF16), 1, 0)
        kv_terms[2 * j + 1] += dot(acts_v, dv.astype(BF16), 1, 0)
        return dk, dv

    def keys_of(source, j, blocks):
        first = pl.multiple_of(ACT + 2 * j * BLOCK, ACT)
        keys = [source[b, pl.ds(first, BLOCK), :] for b in blocks]
        values = [source[b, pl.ds(first + BLOCK, BLOCK), :] for b in blocks]
        if len(blocks) == 1:
            return keys[0], values[0]
        return jnp.concatenate(keys, axis=0), jnp.concatenate(values, axis=0)

    def acts_of(source, blocks):
        sides = [source[b, pl.ds(0, ACT), :] for b in blocks]
        both = sides[0] if len(blocks) == 1 else jnp.concatenate(sides, axis=1)
        return both[:RANK], both[RANK:]

    def own_cases(t, run):
        far = 9 - t

        @pl.when((t == 1) & (z >= 1))
        def _():
            run((1, 0), True)

        @pl.when((t == 1) & (z == 0))
        def _():
            run((0,), True)

        @pl.when((t > 1) & (z >= far))
        def _():
            run((t, far), False)

        @pl.when((t > 1) & (z >= t) & (z < far))
        def _():
            run((t,), False)

    def prev_pair(t):
        second = jnp.where(t == 1, 0, 2 * t - 2)
        return (2 * t - 1, second), (slot(-t), lax.rem(z + t - 1, LINE))

    def own_first(t, first):
        def run(distances, diagonal):
            blocks = [slot(-d) for d in distances]

            def head(j, c):
                keys, values = keys_of(line_kv, j, blocks)
                first_pass(j, keys, values, diagonal)
                return c

            lax.fori_loop(first, first + 2, head, 0)

        own_cases(t, run)

    def prev_first(t):
        indices, blocks = prev_pair(t)
        for index, b in zip(indices, blocks):
            for c, other in ((0, 3), (1, 4)):

                @pl.when(index != other)
                def _():
                    to_next(index, c, b).wait_recv()

        @pl.when(t == 1)
        def _():
            side_right(slot(-1)).start()

        @pl.when(t == 2)
        def _():
            side_left(slot(1)).start()
            side_right(slot(-2)).wait_recv()

        @pl.when(t == 3)
        def _():
            side_left(slot(2)).wait_recv()

        def head(j, c):
            keys, values = keys_of(prev_kv, j, blocks)
            first_pass(j + 2, keys, values, False)
            return c

        lax.fori_loop(0, 2, head, 0)

    def early_step(t):
        block = slot(-t)
        other = slot(t)
        for c in range(2):
            left_e(t, c, other).wait_recv()

            @pl.when(t < 4)
            def _():
                left_e(t + 1, c, other).start()

            @pl.when((t != 2) | (c == 0))
            def _():
                to_next(jnp.minimum(2 * t, LINE - 1), c, other).start()

            @pl.when(t < 4)
            def _():
                right_e(t, c, block).wait_recv()

                @pl.when(t < 3)
                def _():
                    right_e(t + 1, c, block).start()

                @pl.when((t != 2) | (c == 1))
                def _():
                    to_next(2 * t - 1, c, block).start()

    def late_step(t):
        @pl.when(z >= t)
        def _():
            @pl.when(t > 0)
            def _():
                right_l(t, slot(-t)).wait_recv()

            @pl.when((t < 4) & (z < LINE - 1))
            def _():
                right_l(t + 1, slot(-t)).start()

        @pl.when((t < 4) & (slot(t) <= 2))
        def _():
            @pl.when(t > 0)
            def _():
                left_l(t, slot(t)).wait_recv()

            @pl.when(t < 3)
            def _():
                left_l(t + 1, slot(t)).start()

    def begin():
        top[...] = jnp.full(top.shape, HIDDEN, F32)
        total[...] = jnp.zeros(total.shape, F32)
        accum[...] = jnp.zeros(accum.shape, F32)
        dq_t[...] = jnp.zeros(dq_t.shape, F32)
        kv_terms[...] = jnp.zeros(kv_terms.shape, F32)
        for d in range(LINE):
            part[d] = jnp.zeros(part.shape[1:], F32)
        for h in range(KV_HEADS):
            load(q_ref, qs, 0, h).wait()
            load(g_ref, gs, 1, h).wait()

    def gather_step(t, carry):
        early_step(t)

        @pl.when(t == 1)
        def _():
            begin()

        def halves(u, c):
            @pl.when(u == 1)
            def _():
                late_step(t)

            own_first(t, 2 * u)
            return c

        lax.fori_loop(0, 2, halves, 0)

        @pl.when(t > 1)
        def _():
            prev_first(t - 1)

        return carry

    late_step(0)
    lax.fori_loop(1, 5, gather_step, 0)

    def close_rows(first):
        heads = pl.ds(first, 2)
        top[heads] = top[heads] + jnp.log2(total[heads])
        accum[heads] = accum[heads] / total[heads]

    def own_second(t, first):
        def run(distances, diagonal):
            blocks = [slot(-d) for d in distances]
            acts_k, acts_v = acts_of(line_kv, blocks)

            def head(j, c):
                keys, values = keys_of(line_kv, j, blocks)
                dk, dv = second_pass(j, keys, values, acts_k, acts_v, diagonal)
                for i, d in enumerate(distances):
                    rows = slice(i * BLOCK, (i + 1) * BLOCK)
                    part[d, 2 * j] = dk[rows]
                    part[d, 2 * j + 1] = dv[rows]
                return c

            lax.fori_loop(first, first + 2, head, 0)

        own_cases(t, run)

    def prev_second(t):
        indices, blocks = prev_pair(t)
        acts_k, acts_v = acts_of(prev_kv, blocks)

        def head(j, c):
            keys, values = keys_of(prev_kv, j, blocks)
            dk, dv = second_pass(j + 2, keys, values, acts_k, acts_v, False)
            for i, index in enumerate(indices):
                rows = slice(i * BLOCK, (i + 1) * BLOCK)
                prev_part[index, 2 * j] = dk[rows].astype(BF16)
                prev_part[index, 2 * j + 1] = dv[rows].astype(BF16)
            return c

        lax.fori_loop(0, 2, head, 0)
        @pl.when(t == 3)
        def _():
            side_back(1).start()

        @pl.when(t == 2)
        def _():
            side_back(0).start()

        @pl.when(t == 1)
        def _():
            for c, index in ((1, 2), (0, 1)):
                head_rows = pl.ds(2 * c, 2)
                side_back(c).wait_recv()
                prev_part[index, head_rows] = (
                    prev_part[index, head_rows].astype(F32) + side_in[c].astype(F32)
                ).astype(BF16)
            to_prev(2, 1).start()

        for index in indices:
            for c, skipped in ((0, (3,)), (1, (2, 4))):
                sent = index != skipped[0]
                for other in skipped[1:]:
                    sent = sent & (index != other)

                @pl.when(sent)
                def _():
                    to_prev(index, c).start()

    late = pl.ds(4, 4)

    def flush(t):
        ahead = LINE - t

        @pl.when(z >= t)
        def _():
            @pl.when((t < 4) & (z < LINE - 1))
            def _():
                back_left_l(t + 1).wait_recv()
                part[t, late] += left_in[t, late].astype(F32)

            left_out[t - 1, late] = part[t, late].astype(BF16)
            back_left_l(t).start()

        @pl.when((t < 4) & (slot(t) <= 2))
        def _():
            @pl.when(t < 3)
            def _():
                back_right_l(t + 1).wait_recv()
                part[ahead, late] += right_in[t, late].astype(F32)

            right_out[t - 1, late] = part[ahead, late].astype(BF16)
            back_right_l(t).start()

        for c in range(2):
            head = pl.ds(2 * c, 2)

            @pl.when(t < 4)
            def _():
                back_right_e(t + 1, c).wait_recv()
                part[ahead, head] += right_in[t, head].astype(F32)

            index = jnp.minimum(2 * t, LINE - 1)

            @pl.when((t != 2) | (c == 0))
            def _():
                to_prev(index, c).wait_recv()
                part[ahead, head] += next_part[index, head].astype(F32)

            right_out[t - 1, head] = part[ahead, head].astype(BF16)
            back_right_e(t, c).start()

            @pl.when(t < 4)
            def _():
                @pl.when(t < 3)
                def _():
                    back_left_e(t + 1, c).wait_recv()
                    part[t, head] += left_in[t, head].astype(F32)

                @pl.when((t != 2) | (c == 1))
                def _():
                    to_prev(2 * t - 1, c).wait_recv()
                    part[t, head] += next_part[2 * t - 1, head].astype(F32)

                left_out[t - 1, head] = part[t, head].astype(BF16)
                back_left_e(t, c).start()

    close_rows(0)

    def early_second(i, carry):
        own_second(4 - i, 0)
        return carry

    lax.fori_loop(0, AHEAD, early_second, 0)
    prev_first(4)
    close_rows(2)

    def back_step(i, carry):
        t = 5 - i

        @pl.when(t > 1)
        def _():
            prev_second(t - 1)

        @pl.when((i > 1) & (t > 1))
        def _():
            flush(t + 1)

        def halves(u, c):
            @pl.when((i > 0) & ((u == 1) | (i > AHEAD)))
            def _():
                own_second(t, 2 * u)

            return c

        lax.fori_loop(0, 2, halves, 0)

        return carry

    lax.fori_loop(0, 5, back_step, 0)

    def low_block(h, r):
        return (dq_t[places[h], :, pl.ds(r * BLOCK, BLOCK)] * SCALE).astype(BF16)

    for h in range(KV_HEADS):
        for r in range(SHARE):
            term = dot(acts[pl.ds(0, RANK), :], low_block(h, r), 1, 1).astype(BF16)
            c, column = divmod(h * SHARE + r, 4)
            terms[c, :, pl.ds(column * BLOCK, BLOCK)] = term
    for h in range(KV_HEADS):
        terms[h, :, pl.ds(512, BLOCK)] = (kv_terms[2 * places[h]] * SCALE).astype(BF16)
        terms[KV_HEADS + h, :, pl.ds(512, BLOCK)] = kv_terms[2 * places[h] + 1].astype(BF16)

    def stage1_copy(by):
        other = lax.rem(line + by, LINE)
        return copy(
            terms.at[other], stage1.at[by - 1], a_sem1, by - 1, {"ctx": other * LINE + z}
        )

    def stage2_copy(by):
        other = slot(by)
        return copy(
            terms2.at[other // 2], stage2.at[by - 1], a_sem2, by - 1, {"ctx": base + other}
        )

    def stage3_copy(by):
        return copy(terms3, stage3.at[by - 1], a_sem3, by - 1, {"dp": lax.rem(dp + by, 4)})

    for by in range(1, LINE):
        stage1_copy(by).start()
    for h in range(KV_HEADS):
        for r in range(SHARE):
            dq_ref[:, pl.ds((h * SHARE + r) * BLOCK, BLOCK)] = low_block(h, r).T
    flush(2)
    value = terms[line].astype(F32)
    for by in range(1, LINE):
        stage1_copy(by).wait_recv()
        value = value + stage1[by - 1].astype(F32)
    for c in range(4):
        terms2[c, :, pl.ds(0, BLOCK)] = value[:, c * BLOCK : (c + 1) * BLOCK]
        terms2[c, :, pl.ds(BLOCK, BLOCK)] = value[:, 4 * BLOCK :]
    for by in range(1, LINE):
        stage2_copy(by).start()
    flush(1)
    value = terms2[z // 2]
    for by in range(1, LINE):
        stage2_copy(by).wait_recv()
        value = value + stage2[by - 1]
    terms3[...] = value
    for by in range(1, 4):
        stage3_copy(by).start()

    for c in range(2):
        head = pl.ds(2 * c, 2)
        to_prev(0, c).wait_recv()
        back_left_e(1, c).wait_recv()
        back_right_e(1, c).wait_recv()
        final[head] = (
            part[0, head]
            + next_part[0, head].astype(F32)
            + left_in[0, head].astype(F32)
            + right_in[0, head].astype(F32)
        )
    final[late] = part[0, late]

    @pl.when(z < LINE - 1)
    def _():
        back_left_l(1).wait_recv()
        final[late] += left_in[0, late].astype(F32)

    @pl.when(z <= 2)
    def _():
        back_right_l(1).wait_recv()
        final[late] += right_in[0, late].astype(F32)

    for h in range(KV_HEADS):
        span = pl.ds(h * BLOCK, BLOCK)
        dk_ref[:, span] = (final[2 * places[h]] * SCALE).astype(BF16)
        dv_ref[:, span] = final[2 * places[h] + 1].astype(BF16)

    for by in range(1, 4):
        stage3_copy(by).wait_recv()
        value = value + stage3[by - 1]
    q_first = lax.rem(z, 2) * 64 + dp * 16
    kv_first = z * 16 + dp * 4
    aq_ref[...] = pltpu.roll(value[:, :BLOCK], lax.rem(BLOCK - q_first, BLOCK), 1)[:, :RANK]
    columns[...] = value[:, BLOCK:].T
    akv_ref[...] = columns[pl.ds(kv_first, 4), :]

    for s in range(1, 5):
        for c in range(2):
            left_e(s, c, z).wait_send()
            back_right_e(s, c).wait_send()

        @pl.when((z >= s - 1) & (z < LINE - 1))
        def _():
            right_l(s, z).wait_send()

        @pl.when(z >= s)
        def _():
            back_left_l(s).wait_send()

    for s in range(1, 4):
        for c in range(2):
            right_e(s, c, z).wait_send()
            back_left_e(s, c).wait_send()

        @pl.when(slot(s - 1) <= 2)
        def _():
            left_l(s, z).wait_send()

        @pl.when(slot(s) <= 2)
        def _():
            back_right_l(s).wait_send()

    for index in range(LINE):
        for c in range(2):
            if (index, c) not in ((3, 0), (4, 1)):
                to_next(index, c, z).wait_send()
                to_prev(index, c).wait_send()
    side_right(z).wait_send()
    side_left(z).wait_send()
    side_back(0).wait_send()
    side_back(1).wait_send()
    for by in range(1, LINE):
        stage1_copy(by).wait_send()
        stage2_copy(by).wait_send()
    for by in range(1, 4):
        stage3_copy(by).wait_send()


def write_out(*refs):
    count = len(refs) // 2
    for i in range(count):
        refs[count + i][...] = refs[i][...]


def on_device(queries, keys, values, grads_out, ordering, activations):
    count = queries.shape[1]
    vmem = pl.BlockSpec(memory_space=pltpu.VMEM)
    hbm = pl.BlockSpec(memory_space=pltpu.HBM)
    pair = (2 * KV_HEADS, BLOCK, BLOCK)
    half = (KV_HEADS, BLOCK, BLOCK)

    def sems(n):
        return pltpu.SemaphoreType.DMA((2, n))

    shapes = (
        jax.ShapeDtypeStruct((count, queries.shape[2]), BF16),
        jax.ShapeDtypeStruct((count, keys.shape[2]), BF16),
        jax.ShapeDtypeStruct((count, values.shape[2]), BF16),
        jax.ShapeDtypeStruct((RANK, 16), F32),
        jax.ShapeDtypeStruct((4, RANK), F32),
    )
    results = pl.pallas_call(
        kernel,
        out_shape=shapes,
        in_specs=[pl.BlockSpec(memory_space=pltpu.SMEM)] + [hbm] * 5,
        out_specs=(vmem,) * 5,
        scratch_shapes=[
            pltpu.VMEM((KV_HEADS, 2, BLOCK, BLOCK), BF16),
            pltpu.VMEM((LINE, EARLY + HALF, BLOCK), BF16),
            pltpu.VMEM((LINE, EARLY, BLOCK), BF16),
            pltpu.VMEM((KV_HEADS, BLOCK, ROWS), BF16),
            pltpu.VMEM((KV_HEADS, BLOCK, ROWS), BF16),
            pltpu.VMEM((3 * RANK, BLOCK), BF16),
            pltpu.VMEM((KV_HEADS, 1, ROWS), F32),
            pltpu.VMEM((KV_HEADS, 1, ROWS), F32),
            pltpu.VMEM((KV_HEADS, 1, ROWS), F32),
            pltpu.VMEM((2 * BLOCK, ROWS), BF16),
            pltpu.VMEM((2 * BLOCK, ROWS), BF16),
            pltpu.VMEM((KV_HEADS, BLOCK, ROWS), F32),
            pltpu.VMEM((2 * KV_HEADS, RANK, BLOCK), F32),
            pltpu.VMEM((LINE,) + pair, F32),
            pltpu.VMEM((LINE,) + half, BF16),
            pltpu.VMEM((2, 2, BLOCK, BLOCK), BF16),
            pltpu.VMEM((LINE,) + half, BF16),
            pltpu.VMEM((4,) + pair, BF16),
            pltpu.VMEM((4,) + pair, BF16),
            pltpu.VMEM((4,) + pair, BF16),
            pltpu.VMEM((4,) + pair, BF16),
            pltpu.VMEM(pair, F32),
            pltpu.VMEM((LINE, RANK, 5 * BLOCK), BF16),
            pltpu.VMEM((LINE - 1, RANK, 5 * BLOCK), BF16),
            pltpu.VMEM((4, RANK, 2 * BLOCK), F32),
            pltpu.VMEM((LINE - 1, RANK, 2 * BLOCK), F32),
            pltpu.VMEM((RANK, 2 * BLOCK), F32),
            pltpu.VMEM((3, RANK, 2 * BLOCK), F32),
            pltpu.VMEM((BLOCK, RANK), F32),
            sems(KV_HEADS),
            sems(KV_HEADS),
            pltpu.SemaphoreType.DMA((1,)),
            sems(6),
            sems(4),
            sems(8),
            sems(3),
            sems(2 * LINE),
            sems(2),
            sems(2),
            sems(2 * LINE),
            sems(6),
            sems(4),
            sems(8),
            sems(3),
            sems(LINE - 1),
            sems(LINE - 1),
            sems(3),
        ],
        compiler_params=pltpu.CompilerParams(
            collective_id=0, has_side_effects=True, vmem_limit_bytes=62 << 20
        ),
    )(ordering, queries[0], keys[0], values[0], grads_out[0], activations[0].T)
    dq, dk, dv, aq, akv = pl.pallas_call(
        write_out,
        out_shape=shapes,
        in_specs=[vmem] * 5,
        out_specs=(vmem,) * 5,
        compiler_params=pltpu.CompilerParams(vmem_limit_bytes=62 << 20),
    )(*results)
    return dq[None], dk[None], dv[None], aq, akv.T


def solution(mesh):
    placed = (
        P("dp", "ctx", None),
        P("dp", "ctx", None),
        P("dp", "ctx", None),
        P("dp", "ctx", None),
        P("dp", None),
        P("dp", "ctx", None),
    )
    return jax.shard_map(
        on_device,
        mesh=mesh,
        in_specs=placed,
        out_specs=(
            P("dp", "ctx", None),
            P("dp", "ctx", None),
            P("dp", "ctx", None),
            P(None, ("ctx", "dp")),
            P(None, ("ctx", "dp")),
        ),
        check_vma=False,
    )
```

```python
import math

import jax
import jax.numpy as jnp
from jax import lax
from jax.experimental import pallas as pl
from jax.experimental.pallas import tpu as pltpu
from jax.sharding import PartitionSpec as P

MESH = pl.DeviceIdType.MESH
F32 = jnp.float32
BF16 = jnp.bfloat16
BLOCK = 128
FAR_FIRST = (4, 3, 5, 2, 6, 1, 7)
KV_HEADS = 4
SHARE = 8
ROWS = SHARE * BLOCK
AHEAD = 1
LINE = 8
RANK = 16
SCALE = 1.0 / math.sqrt(BLOCK)
EXP2_SCALE = SCALE / math.log(2.0)
HIDDEN = -1e30
ACT = 2 * RANK
HALF = 4 * BLOCK
EARLY = ACT + HALF
CHUNKS = ((0, ACT + 2 * BLOCK), (ACT + 2 * BLOCK, 2 * BLOCK))


def dot(a, b, a_dim, b_dim):
    return lax.dot_general(a, b, (((a_dim,), (b_dim,)), ((), ())), preferred_element_type=F32)


def kernel(
    order_ref,
    q_ref,
    k_ref,
    v_ref,
    g_ref,
    act_ref,
    dq_ref,
    dk_ref,
    dv_ref,
    aq_ref,
    akv_ref,
    own_kv,
    line_kv,
    prev_kv,
    qs,
    gs,
    acts,
    top,
    total,
    accum,
    p_low,
    s_low,
    dq_t,
    kv_terms,
    part,
    prev_part,
    side_in,
    next_part,
    left_out,
    left_in,
    right_out,
    right_in,
    final,
    terms,
    stage1,
    terms2,
    stage2,
    terms3,
    stage3,
    columns,
    load_sem,
    kv_sem,
    act_sem,
    g_right_e,
    g_right_l,
    g_left_e,
    g_left_l,
    g_next,
    g_side,
    b_side,
    b_prev,
    b_left_e,
    b_left_l,
    b_right_e,
    b_right_l,
    a_sem1,
    a_sem2,
    a_sem3,
):
    ctx = lax.axis_index("ctx")
    dp = lax.axis_index("dp")
    z = lax.rem(ctx, LINE)
    line = ctx // LINE
    base = line * LINE
    left = base + lax.rem(z + LINE - 1, LINE)
    right = base + lax.rem(z + 1, LINE)
    after = lax.rem(line + 1, LINE) * LINE + z
    before = lax.rem(line + LINE - 1, LINE) * LINE + z

    def copy(src, dst, sems, index, target):
        return pltpu.make_async_remote_copy(
            src_ref=src,
            dst_ref=dst,
            send_sem=sems.at[0, index],
            recv_sem=sems.at[1, index],
            device_id=target,
            device_id_type=MESH,
        )

    def slot(by):
        return lax.rem(z + by + LINE, LINE)

    def right_e(s, c, block):
        view = line_kv.at[block, pl.ds(*CHUNKS[c])]
        return copy(view, view, g_right_e, 2 * (s - 1) + c, {"ctx": right})

    def right_l(s, block):
        view = line_kv.at[block, pl.ds(EARLY, HALF)]
        return copy(view, view, g_right_l, s - 1, {"ctx": right})

    def left_e(s, c, block):
        view = line_kv.at[block, pl.ds(*CHUNKS[c])]
        return copy(view, view, g_left_e, 2 * (s - 1) + c, {"ctx": left})

    def left_l(s, block):
        view = line_kv.at[block, pl.ds(EARLY, HALF)]
        return copy(view, view, g_left_l, s - 1, {"ctx": left})

    def to_next(index, c, block):
        rows = pl.ds(*CHUNKS[c])
        return copy(
            line_kv.at[block, rows],
            prev_kv.at[block, rows],
            g_next,
            2 * index + c,
            {"ctx": after},
        )

    def side_right(block):
        view = prev_kv.at[block, pl.ds(*CHUNKS[0])]
        return copy(view, view, g_side, 0, {"ctx": right})

    def side_left(block):
        view = prev_kv.at[block, pl.ds(*CHUNKS[1])]
        return copy(view, view, g_side, 1, {"ctx": left})

    def side_back(c):
        index, target = ((3, left), (4, right))[c]
        return copy(
            prev_part.at[index, pl.ds(2 * c, 2)], side_in.at[c], b_side, c, {"ctx": target}
        )

    def to_prev(index, c):
        view = pl.ds(2 * c, 2)
        return copy(
            prev_part.at[index, view],
            next_part.at[index, view],
            b_prev,
            2 * index + c,
            {"ctx": before},
        )

    def back_left_e(s, c):
        view = pl.ds(2 * c, 2)
        return copy(
            left_out.at[s - 1, view],
            left_in.at[s - 1, view],
            b_left_e,
            2 * (s - 1) + c,
            {"ctx": left},
        )

    def back_right_e(s, c):
        view = pl.ds(2 * c, 2)
        return copy(
            right_out.at[s - 1, view],
            right_in.at[s - 1, view],
            b_right_e,
            2 * (s - 1) + c,
            {"ctx": right},
        )

    def back_left_l(s):
        return copy(
            left_out.at[s - 1, pl.ds(4, 4)],
            left_in.at[s - 1, pl.ds(4, 4)],
            b_left_l,
            s - 1,
            {"ctx": left},
        )

    def back_right_l(s):
        return copy(
            right_out.at[s - 1, pl.ds(4, 4)],
            right_in.at[s - 1, pl.ds(4, 4)],
            b_right_l,
            s - 1,
            {"ctx": right},
        )

    def load(src, dst, row, h):
        return pltpu.make_async_copy(
            src.at[:, pl.ds(h * ROWS, ROWS)], dst.at[h], load_sem.at[row, h]
        )

    def load_kv(src, which, h):
        return pltpu.make_async_copy(
            src.at[:, pl.ds(h * BLOCK, BLOCK)], own_kv.at[h, which], kv_sem.at[which, h]
        )

    barrier = pltpu.get_barrier_semaphore()
    for by in range(1, LINE):
        pl.semaphore_signal(barrier, inc=1, device_id={"ctx": base + slot(by)}, device_id_type=MESH)
        pl.semaphore_signal(
            barrier,
            inc=1,
            device_id={"ctx": lax.rem(line + by, LINE) * LINE + z},
            device_id_type=MESH,
        )
    for by in range(1, 4):
        pl.semaphore_signal(
            barrier, inc=1, device_id={"dp": lax.rem(dp + by, 4)}, device_id_type=MESH
        )

    load_act = pltpu.make_async_copy(act_ref, acts, act_sem.at[0])
    for h in range(KV_HEADS):
        load_kv(k_ref, 0, h).start()
        load_kv(v_ref, 1, h).start()
    load_act.start()

    swap = 2 * (1 - lax.rem(line, 2))
    ordering = [order_ref[0, lax.rem(j + swap, KV_HEADS)] for j in range(KV_HEADS)]
    places = []
    for h in range(KV_HEADS):
        place = jnp.int32(0)
        for j in range(1, KV_HEADS):
            place = jnp.maximum(place, jnp.where(ordering[j] == h, j, 0))
        places.append(place)

    for h in range(KV_HEADS):
        load_kv(k_ref, 0, h).wait()
        load_kv(v_ref, 1, h).wait()
    load_act.wait()
    line_kv[z, pl.ds(0, ACT), :] = acts[pl.ds(RANK, ACT), :]
    for j in range(KV_HEADS):
        first = ACT + 2 * j * BLOCK
        line_kv[z, pl.ds(first, BLOCK), :] = own_kv[ordering[j], 0]
        line_kv[z, pl.ds(first + BLOCK, BLOCK), :] = own_kv[ordering[j], 1]

    pl.semaphore_wait(barrier, 2 * (LINE - 1) + 3)
    for c in range(2):
        left_e(1, c, z).start()
        right_e(1, c, z).start()
        to_next(0, c, z).start()

    for h in range(KV_HEADS):
        load(q_ref, qs, 0, h).start()
        load(g_ref, gs, 1, h).start()

    width = 2 * BLOCK

    def name(j):
        return order_ref[0, lax.rem(j + swap, KV_HEADS)]

    def rows_of(source, j, first, count):
        heads = [source[name(j), :, pl.ds(r * BLOCK, BLOCK)] for r in range(first, first + count)]
        return jnp.concatenate(heads, axis=0)

    def scores(j, piece, keys, diagonal):
        q = rows_of(qs, j, 2 * piece, 2)
        s = dot(keys, q, 1, 1) * EXP2_SCALE
        if diagonal:
            key_at = lax.broadcasted_iota(jnp.int32, (BLOCK, width), 0)
            query_at = lax.rem(lax.broadcasted_iota(jnp.int32, (BLOCK, width), 1), BLOCK)
            own = jnp.where(key_at <= query_at, s[-BLOCK:], HIDDEN)
            s = own if s.shape[0] == BLOCK else jnp.concatenate([s[:-BLOCK], own], axis=0)
        return s

    def first_pass(j, keys, values, diagonal):
        for piece in range(ROWS // width):
            cols = pl.ds(piece * width, width)
            s = scores(j, piece, keys, diagonal)
            old = top[j, :, cols]
            new = jnp.maximum(old, jnp.max(s, axis=0, keepdims=True))
            e = jnp.exp2(s - new)
            dp_ = dot(values, rows_of(gs, j, 2 * piece, 2), 1, 1)
            factor = jnp.exp2(old - new)
            total[j, :, cols] = total[j, :, cols] * factor + jnp.sum(e, axis=0, keepdims=True)
            accum[j, :, cols] = accum[j, :, cols] * factor + jnp.sum(e * dp_, axis=0, keepdims=True)
            top[j, :, cols] = new

    def second_pass(j, keys, values, acts_k, acts_v, diagonal):
        count = keys.shape[0]
        for piece in range(ROWS // width):
            cols = pl.ds(piece * width, width)
            p = jnp.exp2(scores(j, piece, keys, diagonal) - top[j, :, cols])
            dp_ = dot(values, rows_of(gs, j, 2 * piece, 2), 1, 1)
            s_low[pl.ds(0, count), cols] = (p * (dp_ - accum[j, :, cols])).astype(BF16)
            p_low[pl.ds(0, count), cols] = p.astype(BF16)
        ds = s_low[pl.ds(0, count), :]
        dk = dot(ds, rows_of(qs, j, 0, SHARE), 1, 0)
        dv = dot(p_low[pl.ds(0, count), :], rows_of(gs, j, 0, SHARE), 1, 0)
        dq_t[j] += dot(keys, ds, 0, 0)
        kv_terms[2 * j] += dot(acts_k, dk.astype(BF16), 1, 0)
        kv_terms[2 * j + 1] += dot(acts_v, dv.astype(BF16), 1, 0)
        return dk, dv

    def keys_of(source, j, blocks):
        first = pl.multiple_of(ACT + 2 * j * BLOCK, ACT)
        keys = [source[b, pl.ds(first, BLOCK), :] for b in blocks]
        values = [source[b, pl.ds(first + BLOCK, BLOCK), :] for b in blocks]
        if len(blocks) == 1:
            return keys[0], values[0]
        return jnp.concatenate(keys, axis=0), jnp.concatenate(values, axis=0)

    def acts_of(source, blocks):
        sides = [source[b, pl.ds(0, ACT), :] for b in blocks]
        both = sides[0] if len(blocks) == 1 else jnp.concatenate(sides, axis=1)
        return both[:RANK], both[RANK:]

    def own_cases(t, run):
        far = 9 - t

        @pl.when((t == 1) & (z >= 1))
        def _():
            run((1, 0), True)

        @pl.when((t == 1) & (z == 0))
        def _():
            run((0,), True)

        @pl.when((t > 1) & (z >= far))
        def _():
            run((t, far), False)

        @pl.when((t > 1) & (z >= t) & (z < far))
        def _():
            run((t,), False)

    def prev_pair(t):
        second = jnp.where(t == 1, 0, 2 * t - 2)
        return (2 * t - 1, second), (slot(-t), lax.rem(z + t - 1, LINE))

    def own_first(t, first):
        def run(distances, diagonal):
            blocks = [slot(-d) for d in distances]

            def head(j, c):
                keys, values = keys_of(line_kv, j, blocks)
                first_pass(j, keys, values, diagonal)
                return c

            lax.fori_loop(first, first + 2, head, 0)

        own_cases(t, run)

    def prev_first(t):
        indices, blocks = prev_pair(t)
        for index, b in zip(indices, blocks):
            for c, other in ((0, 3), (1, 4)):

                @pl.when(index != other)
                def _():
                    to_next(index, c, b).wait_recv()

        @pl.when(t == 1)
        def _():
            side_right(slot(-1)).start()

        @pl.when(t == 2)
        def _():
            side_left(slot(1)).start()
            side_right(slot(-2)).wait_recv()

        @pl.when(t == 3)
        def _():
            side_left(slot(2)).wait_recv()

        def head(j, c):
            keys, values = keys_of(prev_kv, j, blocks)
            first_pass(j + 2, keys, values, False)
            return c

        lax.fori_loop(0, 2, head, 0)

    def early_step(t):
        block = slot(-t)
        other = slot(t)
        for c in range(2):
            left_e(t, c, other).wait_recv()

            @pl.when(t < 4)
            def _():
                left_e(t + 1, c, other).start()

            @pl.when((t != 2) | (c == 0))
            def _():
                to_next(jnp.minimum(2 * t, LINE - 1), c, other).start()

            @pl.when(t < 4)
            def _():
                right_e(t, c, block).wait_recv()

                @pl.when(t < 3)
                def _():
                    right_e(t + 1, c, block).start()

                @pl.when((t != 2) | (c == 1))
                def _():
                    to_next(2 * t - 1, c, block).start()

    def late_step(t):
        @pl.when(z >= t)
        def _():
            @pl.when(t > 0)
            def _():
                right_l(t, slot(-t)).wait_recv()

            @pl.when((t < 4) & (z < LINE - 1))
            def _():
                right_l(t + 1, slot(-t)).start()

        @pl.when((t < 4) & (slot(t) <= 2))
        def _():
            @pl.when(t > 0)
            def _():
                left_l(t, slot(t)).wait_recv()

            @pl.when(t < 3)
            def _():
                left_l(t + 1, slot(t)).start()

    def begin():
        top[...] = jnp.full(top.shape, HIDDEN, F32)
        total[...] = jnp.zeros(total.shape, F32)
        accum[...] = jnp.zeros(accum.shape, F32)
        dq_t[...] = jnp.zeros(dq_t.shape, F32)
        kv_terms[...] = jnp.zeros(kv_terms.shape, F32)
        for d in range(LINE):
            part[d] = jnp.zeros(part.shape[1:], F32)
        for h in range(KV_HEADS):
            load(q_ref, qs, 0, h).wait()
            load(g_ref, gs, 1, h).wait()

    def gather_step(t, carry):
        early_step(t)

        @pl.when(t == 1)
        def _():
            begin()

        def halves(u, c):
            @pl.when(u == 1)
            def _():
                late_step(t)

            own_first(t, 2 * u)
            return c

        lax.fori_loop(0, 2, halves, 0)

        @pl.when(t > 1)
        def _():
            prev_first(t - 1)

        return carry

    late_step(0)
    lax.fori_loop(1, 5, gather_step, 0)

    def close_rows(first):
        heads = pl.ds(first, 2)
        top[heads] = top[heads] + jnp.log2(total[heads])
        accum[heads] = accum[heads] / total[heads]

    def own_second(t, first):
        def run(distances, diagonal):
            blocks = [slot(-d) for d in distances]
            acts_k, acts_v = acts_of(line_kv, blocks)

            def head(j, c):
                keys, values = keys_of(line_kv, j, blocks)
                dk, dv = second_pass(j, keys, values, acts_k, acts_v, diagonal)
                for i, d in enumerate(distances):
                    rows = slice(i * BLOCK, (i + 1) * BLOCK)
                    part[d, 2 * j] = dk[rows]
                    part[d, 2 * j + 1] = dv[rows]
                return c

            lax.fori_loop(first, first + 2, head, 0)

        own_cases(t, run)

    def prev_second(t):
        indices, blocks = prev_pair(t)
        acts_k, acts_v = acts_of(prev_kv, blocks)

        def head(j, c):
            keys, values = keys_of(prev_kv, j, blocks)
            dk, dv = second_pass(j + 2, keys, values, acts_k, acts_v, False)
            for i, index in enumerate(indices):
                rows = slice(i * BLOCK, (i + 1) * BLOCK)
                prev_part[index, 2 * j] = dk[rows].astype(BF16)
                prev_part[index, 2 * j + 1] = dv[rows].astype(BF16)
            return c

        lax.fori_loop(0, 2, head, 0)
        @pl.when(t == 3)
        def _():
            side_back(1).start()

        @pl.when(t == 2)
        def _():
            side_back(0).start()

        @pl.when(t == 1)
        def _():
            for c, index in ((1, 2), (0, 1)):
                head_rows = pl.ds(2 * c, 2)
                side_back(c).wait_recv()
                prev_part[index, head_rows] = (
                    prev_part[index, head_rows].astype(F32) + side_in[c].astype(F32)
                ).astype(BF16)
            to_prev(2, 1).start()

        for index in indices:
            for c, skipped in ((0, (3,)), (1, (2, 4))):
                sent = index != skipped[0]
                for other in skipped[1:]:
                    sent = sent & (index != other)

                @pl.when(sent)
                def _():
                    to_prev(index, c).start()

    late = pl.ds(4, 4)

    def flush(t):
        ahead = LINE - t

        @pl.when(z >= t)
        def _():
            @pl.when((t < 4) & (z < LINE - 1))
            def _():
                back_left_l(t + 1).wait_recv()
                part[t, late] += left_in[t, late].astype(F32)

            left_out[t - 1, late] = part[t, late].astype(BF16)
            back_left_l(t).start()

        @pl.when((t < 4) & (slot(t) <= 2))
        def _():
            @pl.when(t < 3)
            def _():
                back_right_l(t + 1).wait_recv()
                part[ahead, late] += right_in[t, late].astype(F32)

            right_out[t - 1, late] = part[ahead, late].astype(BF16)
            back_right_l(t).start()

        for c in range(2):
            head = pl.ds(2 * c, 2)

            @pl.when(t < 4)
            def _():
                back_right_e(t + 1, c).wait_recv()
                part[ahead, head] += right_in[t, head].astype(F32)

            index = jnp.minimum(2 * t, LINE - 1)

            @pl.when((t != 2) | (c == 0))
            def _():
                to_prev(index, c).wait_recv()
                part[ahead, head] += next_part[index, head].astype(F32)

            right_out[t - 1, head] = part[ahead, head].astype(BF16)
            back_right_e(t, c).start()

            @pl.when(t < 4)
            def _():
                @pl.when(t < 3)
                def _():
                    back_left_e(t + 1, c).wait_recv()
                    part[t, head] += left_in[t, head].astype(F32)

                @pl.when((t != 2) | (c == 1))
                def _():
                    to_prev(2 * t - 1, c).wait_recv()
                    part[t, head] += next_part[2 * t - 1, head].astype(F32)

                left_out[t - 1, head] = part[t, head].astype(BF16)
                back_left_e(t, c).start()

    close_rows(0)

    def early_second(i, carry):
        own_second(4 - i, 0)
        return carry

    lax.fori_loop(0, AHEAD, early_second, 0)
    prev_first(4)
    close_rows(2)

    def back_step(i, carry):
        t = 5 - i

        @pl.when(t > 1)
        def _():
            prev_second(t - 1)

        @pl.when((i > 1) & (t > 1))
        def _():
            flush(t + 1)

        def halves(u, c):
            @pl.when((i > 0) & ((u == 1) | (i > AHEAD)))
            def _():
                own_second(t, 2 * u)

            return c

        lax.fori_loop(0, 2, halves, 0)

        return carry

    lax.fori_loop(0, 5, back_step, 0)

    def low_block(h, r):
        return (dq_t[places[h], :, pl.ds(r * BLOCK, BLOCK)] * SCALE).astype(BF16)

    for h in range(KV_HEADS):
        for r in range(SHARE):
            term = dot(acts[pl.ds(0, RANK), :], low_block(h, r), 1, 1).astype(BF16)
            c, column = divmod(h * SHARE + r, 4)
            terms[c, :, pl.ds(column * BLOCK, BLOCK)] = term
    for h in range(KV_HEADS):
        terms[h, :, pl.ds(512, BLOCK)] = (kv_terms[2 * places[h]] * SCALE).astype(BF16)
        terms[KV_HEADS + h, :, pl.ds(512, BLOCK)] = kv_terms[2 * places[h] + 1].astype(BF16)

    def stage1_copy(by):
        other = lax.rem(line + by, LINE)
        return copy(
            terms.at[other], stage1.at[by - 1], a_sem1, by - 1, {"ctx": other * LINE + z}
        )

    def stage2_copy(by):
        other = slot(by)
        return copy(
            terms2.at[other // 2], stage2.at[by - 1], a_sem2, by - 1, {"ctx": base + other}
        )

    def stage3_copy(by):
        return copy(terms3, stage3.at[by - 1], a_sem3, by - 1, {"dp": lax.rem(dp + by, 4)})

    for by in FAR_FIRST:
        stage1_copy(by).start()
    for h in range(KV_HEADS):
        for r in range(SHARE):
            dq_ref[:, pl.ds((h * SHARE + r) * BLOCK, BLOCK)] = low_block(h, r).T
    flush(2)
    value = terms[line].astype(F32)
    for by in range(1, LINE):
        stage1_copy(by).wait_recv()
        value = value + stage1[by - 1].astype(F32)
    for c in range(4):
        terms2[c, :, pl.ds(0, BLOCK)] = value[:, c * BLOCK : (c + 1) * BLOCK]
        terms2[c, :, pl.ds(BLOCK, BLOCK)] = value[:, 4 * BLOCK :]
    for by in FAR_FIRST:
        stage2_copy(by).start()
    flush(1)
    value = terms2[z // 2]
    for by in range(1, LINE):
        stage2_copy(by).wait_recv()
        value = value + stage2[by - 1]
    terms3[...] = value
    for by in range(1, 4):
        stage3_copy(by).start()

    for c in range(2):
        head = pl.ds(2 * c, 2)
        to_prev(0, c).wait_recv()
        back_left_e(1, c).wait_recv()
        back_right_e(1, c).wait_recv()
        final[head] = (
            part[0, head]
            + next_part[0, head].astype(F32)
            + left_in[0, head].astype(F32)
            + right_in[0, head].astype(F32)
        )
    final[late] = part[0, late]

    @pl.when(z < LINE - 1)
    def _():
        back_left_l(1).wait_recv()
        final[late] += left_in[0, late].astype(F32)

    @pl.when(z <= 2)
    def _():
        back_right_l(1).wait_recv()
        final[late] += right_in[0, late].astype(F32)

    for h in range(KV_HEADS):
        span = pl.ds(h * BLOCK, BLOCK)
        dk_ref[:, span] = (final[2 * places[h]] * SCALE).astype(BF16)
        dv_ref[:, span] = final[2 * places[h] + 1].astype(BF16)

    for by in range(1, 4):
        stage3_copy(by).wait_recv()
        value = value + stage3[by - 1]
    q_first = lax.rem(z, 2) * 64 + dp * 16
    kv_first = z * 16 + dp * 4
    aq_ref[...] = pltpu.roll(value[:, :BLOCK], lax.rem(BLOCK - q_first, BLOCK), 1)[:, :RANK]
    columns[...] = value[:, BLOCK:].T
    akv_ref[...] = columns[pl.ds(kv_first, 4), :]

    for s in range(1, 5):
        for c in range(2):
            left_e(s, c, z).wait_send()
            back_right_e(s, c).wait_send()

        @pl.when((z >= s - 1) & (z < LINE - 1))
        def _():
            right_l(s, z).wait_send()

        @pl.when(z >= s)
        def _():
            back_left_l(s).wait_send()

    for s in range(1, 4):
        for c in range(2):
            right_e(s, c, z).wait_send()
            back_left_e(s, c).wait_send()

        @pl.when(slot(s - 1) <= 2)
        def _():
            left_l(s, z).wait_send()

        @pl.when(slot(s) <= 2)
        def _():
            back_right_l(s).wait_send()

    for index in range(LINE):
        for c in range(2):
            if (index, c) not in ((3, 0), (4, 1)):
                to_next(index, c, z).wait_send()
                to_prev(index, c).wait_send()
    side_right(z).wait_send()
    side_left(z).wait_send()
    side_back(0).wait_send()
    side_back(1).wait_send()
    for by in range(1, LINE):
        stage1_copy(by).wait_send()
        stage2_copy(by).wait_send()
    for by in range(1, 4):
        stage3_copy(by).wait_send()


def write_out(*refs):
    count = len(refs) // 2
    for i in range(count):
        refs[count + i][...] = refs[i][...]


def on_device(queries, keys, values, grads_out, ordering, activations):
    count = queries.shape[1]
    vmem = pl.BlockSpec(memory_space=pltpu.VMEM)
    hbm = pl.BlockSpec(memory_space=pltpu.HBM)
    pair = (2 * KV_HEADS, BLOCK, BLOCK)
    half = (KV_HEADS, BLOCK, BLOCK)

    def sems(n):
        return pltpu.SemaphoreType.DMA((2, n))

    shapes = (
        jax.ShapeDtypeStruct((count, queries.shape[2]), BF16),
        jax.ShapeDtypeStruct((count, keys.shape[2]), BF16),
        jax.ShapeDtypeStruct((count, values.shape[2]), BF16),
        jax.ShapeDtypeStruct((RANK, 16), F32),
        jax.ShapeDtypeStruct((4, RANK), F32),
    )
    results = pl.pallas_call(
        kernel,
        out_shape=shapes,
        in_specs=[pl.BlockSpec(memory_space=pltpu.SMEM)] + [hbm] * 5,
        out_specs=(vmem,) * 5,
        scratch_shapes=[
            pltpu.VMEM((KV_HEADS, 2, BLOCK, BLOCK), BF16),
            pltpu.VMEM((LINE, EARLY + HALF, BLOCK), BF16),
            pltpu.VMEM((LINE, EARLY, BLOCK), BF16),
            pltpu.VMEM((KV_HEADS, BLOCK, ROWS), BF16),
            pltpu.VMEM((KV_HEADS, BLOCK, ROWS), BF16),
            pltpu.VMEM((3 * RANK, BLOCK), BF16),
            pltpu.VMEM((KV_HEADS, 1, ROWS), F32),
            pltpu.VMEM((KV_HEADS, 1, ROWS), F32),
            pltpu.VMEM((KV_HEADS, 1, ROWS), F32),
            pltpu.VMEM((2 * BLOCK, ROWS), BF16),
            pltpu.VMEM((2 * BLOCK, ROWS), BF16),
            pltpu.VMEM((KV_HEADS, BLOCK, ROWS), F32),
            pltpu.VMEM((2 * KV_HEADS, RANK, BLOCK), F32),
            pltpu.VMEM((LINE,) + pair, F32),
            pltpu.VMEM((LINE,) + half, BF16),
            pltpu.VMEM((2, 2, BLOCK, BLOCK), BF16),
            pltpu.VMEM((LINE,) + half, BF16),
            pltpu.VMEM((4,) + pair, BF16),
            pltpu.VMEM((4,) + pair, BF16),
            pltpu.VMEM((4,) + pair, BF16),
            pltpu.VMEM((4,) + pair, BF16),
            pltpu.VMEM(pair, F32),
            pltpu.VMEM((LINE, RANK, 5 * BLOCK), BF16),
            pltpu.VMEM((LINE - 1, RANK, 5 * BLOCK), BF16),
            pltpu.VMEM((4, RANK, 2 * BLOCK), F32),
            pltpu.VMEM((LINE - 1, RANK, 2 * BLOCK), F32),
            pltpu.VMEM((RANK, 2 * BLOCK), F32),
            pltpu.VMEM((3, RANK, 2 * BLOCK), F32),
            pltpu.VMEM((BLOCK, RANK), F32),
            sems(KV_HEADS),
            sems(KV_HEADS),
            pltpu.SemaphoreType.DMA((1,)),
            sems(6),
            sems(4),
            sems(8),
            sems(3),
            sems(2 * LINE),
            sems(2),
            sems(2),
            sems(2 * LINE),
            sems(6),
            sems(4),
            sems(8),
            sems(3),
            sems(LINE - 1),
            sems(LINE - 1),
            sems(3),
        ],
        compiler_params=pltpu.CompilerParams(
            collective_id=0, has_side_effects=True, vmem_limit_bytes=62 << 20
        ),
    )(ordering, queries[0], keys[0], values[0], grads_out[0], activations[0].T)
    dq, dk, dv, aq, akv = pl.pallas_call(
        write_out,
        out_shape=shapes,
        in_specs=[vmem] * 5,
        out_specs=(vmem,) * 5,
        compiler_params=pltpu.CompilerParams(vmem_limit_bytes=62 << 20),
    )(*results)
    return dq[None], dk[None], dv[None], aq, akv.T


def solution(mesh):
    placed = (
        P("dp", "ctx", None),
        P("dp", "ctx", None),
        P("dp", "ctx", None),
        P("dp", "ctx", None),
        P("dp", None),
        P("dp", "ctx", None),
    )
    return jax.shard_map(
        on_device,
        mesh=mesh,
        in_specs=placed,
        out_specs=(
            P("dp", "ctx", None),
            P("dp", "ctx", None),
            P("dp", "ctx", None),
            P(None, ("ctx", "dp")),
            P(None, ("ctx", "dp")),
        ),
        check_vma=False,
    )
```
